512 devices in a mesh: dp: 16 (over x, y_hi), section: 4 (over y_lo, core), tensor: 8 (over z).
Axes of the slice: x: 4, y: 8 (y_hi: 4, y_lo: 2; y = y_hi * 2 + y_lo), z: 8, core: 2. Of those that a mesh axis runs over, the one named last changes fastest.
Arguments:
- latents: bfloat16 [640, 32, 256], P('tensor', 'dp'), may hold values from -40 to 40
- target: bfloat16 [640, 32, 256], P('tensor', 'dp'), may hold values from -6 to 6
- base_weight: bfloat16 [4, 640, 9, 640], P('section', 'tensor'), may hold values from -0.078125 to 0.078125
- seeds: int32 [4], P('section'), may hold values from 0 to 65520
- timesteps: int32 [32], P('dp'), may hold values from 0 to 999
- time_table: bfloat16 [4, 1000, 640], P('section', None, 'tensor'), may hold values from -4 to 4
Outputs:
- weight_grad: float32 [4, 640, 9, 640], P('section', 'tensor')
The draws below stay inside these ranges and needn't reach their ends.
All inputs are finite; a program needn't handle non-finite values.
Results may differ from the reference program's by a relative error of at most 0.006.
Values may be sent and summed in bfloat16 or wider, within the bound.
A program may use at most 64 MiB of HBM per device.

```python
import math
import jax
import jax.numpy as jnp
from jax import lax

C = 640
GROUPS = 32
RES = 16
NT = 1000
SECTIONS = 4
LATENTS = 32


def draw_latents(key, part):
    key = jax.random.fold_in(key, 1)
    key_base, key_chan, key_pixel = jax.random.split(key, 3)
    shape_all = (C, LATENTS, RES * RES)
    chan_scale = jnp.exp(jax.random.uniform(key_chan, (C, 1, 1), jnp.float32, 0.0, math.log(10.0)))
    pixel_scale = jnp.exp(jax.random.uniform(key_pixel, (1, LATENTS, RES * RES), jnp.float32, 0.0, math.log(10.0)))
    scale_both = chan_scale * pixel_scale / 10.0
    values = jax.random.truncated_normal(key_base, -4.0, 4.0, shape_all, jnp.float32)
    return (values * scale_both).astype(jnp.bfloat16)


def plant(result, key, smallest, top_value):
    shape = result.shape
    place = [jax.random.randint(jax.random.fold_in(key, axis), (), 0, shape[axis]) for axis in range(len(shape))]
    result = result.at[tuple(place)].set(smallest)
    longest = shape.index(max(shape))
    place[longest] = (place[longest] + 1) % shape[longest]
    return result.at[tuple(place)].set(top_value)


def block_scale(key, shape, cuts, low, top_value):
    factor_of = 1.0
    for position, blocks in cuts:
        steps = jax.random.uniform(jax.random.fold_in(jax.random.fold_in(key, 6), position), (blocks,), jnp.float32, low / len(cuts), top_value / len(cuts))
        factor_of = factor_of * jnp.repeat(jnp.exp(steps), shape[position] // blocks).reshape((-1,) + (1,) * (len(shape) - 1 - position))
    return factor_of


def normal_values(own_key, shape, spread, reach, cuts=(), held_as=jnp.bfloat16):
    gain = block_scale(own_key, shape, cuts, -0.22, 0.18) if cuts else 1.0
    result = jax.random.normal(own_key, shape, jnp.float32) * spread * gain
    return jnp.minimum(jnp.maximum(result, -reach), reach).astype(held_as)


def setup_inputs(seed: int = 0) -> dict:
    arg_keys = jax.random.split(jax.random.key(seed), 7)
    latents = draw_latents(jax.random.fold_in(arg_keys[6], 71), 0)
    target = normal_values(arg_keys[1], (C, LATENTS, RES * RES), 1.0, 6.0, ((0, 8), (1, 16)))
    base_weight = normal_values(arg_keys[2], (SECTIONS, C, 9, C), (9 * C) ** -0.5, 0.078125, ((0, 4), (1, 8)))
    seeds = plant(jax.random.randint(arg_keys[3], (SECTIONS,), 0, 65521), jax.random.fold_in(arg_keys[3], 1), 0, 65520).astype(jnp.int32)
    timesteps = plant(jax.random.randint(arg_keys[4], (LATENTS,), 0, NT), jax.random.fold_in(arg_keys[4], 1), 0, NT - 1).astype(jnp.int32)
    time_table = normal_values(arg_keys[5], (SECTIONS, NT, C), 0.5, 4.0, ((0, 4), (2, 8)))
    return dict(latents=latents, target=target, base_weight=base_weight, seeds=seeds, timesteps=timesteps, time_table=time_table)


noise_scale = 0.02

def noise(seed_value, first_row, row_count, col_count):
    shape_all = (row_count, 9, col_count)
    channel = lax.broadcasted_iota(jnp.int32, shape_all, 0) + first_row
    kernel_tap = lax.broadcasted_iota(jnp.int32, shape_all, 1)
    out_channel = lax.broadcasted_iota(jnp.int32, shape_all, 2)
    flat_index = (channel * 9 + kernel_tap) * col_count + out_channel
    low_part = flat_index % 65521
    high_part = flat_index // 65521
    hashed = (low_part * 32749 + high_part * 12345 + seed_value) % 65521
    return hashed.astype(jnp.float32) / 65521.0 - 0.5

def activate(inputs, bias_vec, group_size):
    shifted = inputs + bias_vec[:, None]
    channels = shifted.shape[0]
    pixels = shifted.shape[1]
    grouped = shifted.reshape(channels // group_size, group_size * pixels)
    center = grouped - lax.optimization_barrier(jnp.mean(grouped, axis=1, keepdims=True))
    normed = center * lax.rsqrt(lax.optimization_barrier(jnp.mean(center * center, axis=1, keepdims=True)) + 1e-05)
    return jax.nn.silu(normed.reshape(channels, pixels))

def unfold(activation, side_len):
    channels = activation.shape[0]
    image_grid = activation.reshape(channels, side_len, side_len)
    padded = jnp.pad(image_grid, ((0, 0), (1, 1), (1, 1)))
    tap_list = [padded[:, shift_row:shift_row + side_len, shift_col:shift_col + side_len] for shift_row in range(3) for shift_col in range(3)]
    return jnp.stack(tap_list, axis=1).reshape(channels, 9, side_len * side_len)

def fold_back(columns, side_len):
    channels = columns.shape[0]
    tap_parts = columns.reshape(channels, 9, side_len, side_len)
    padded = jnp.zeros((channels, side_len + 2, side_len + 2), jnp.float32)
    for shift_row in range(3):
        for shift_col in range(3):
            padded = padded.at[:, shift_row:shift_row + side_len, shift_col:shift_col + side_len].add(tap_parts[:, shift_row * 3 + shift_col])
    return padded[:, 1:-1, 1:-1].reshape(channels, side_len * side_len)

def forward_block(section_input, weight, step_bias):
    inputs = section_input.astype(jnp.float32)
    activation = activate(inputs, step_bias, C // GROUPS).astype(jnp.bfloat16)
    columns = unfold(activation, RES).astype(jnp.float32)
    conv_sum = jnp.einsum('cko,ckp->op', weight.astype(jnp.float32), columns, precision=lax.Precision.HIGHEST)
    return (inputs + step_bias[:, None] + conv_sum).astype(jnp.bfloat16)

def backward_block(section_input, out_grad, weight, step_bias):
    act_value, act_back = jax.vjp(lambda values: activate(values, step_bias, C // GROUPS), section_input.astype(jnp.float32))
    columns = unfold(act_value.astype(jnp.bfloat16), RES).astype(jnp.float32)
    grad_float = out_grad.astype(jnp.float32)
    weight_part = jnp.einsum('ckp,op->cko', columns, grad_float, precision=lax.Precision.HIGHEST)
    col_grad = jnp.einsum('cko,op->ckp', weight.astype(jnp.float32), grad_float, precision=lax.Precision.HIGHEST)
    input_grad = act_back(fold_back(col_grad, RES))[0]
    return (weight_part, (grad_float + input_grad).astype(jnp.bfloat16))

def reference(latents, target, base_weight, seeds, timesteps, time_table):
    section_weights = [(base_weight[section_number].astype(jnp.float32) + noise_scale * noise(seeds[section_number], 0, C, C)).astype(jnp.bfloat16) for section_number in range(SECTIONS)]

    def one_latent(totals, latent_index):
        hidden_state = latents[:, latent_index]
        step_value = timesteps[latent_index]
        section_inputs = []
        biases = []
        for section_number in range(SECTIONS):
            step_bias = time_table[section_number, step_value].astype(jnp.float32)
            biases.append(step_bias)
            section_inputs.append(hidden_state)
            hidden_state = forward_block(hidden_state, section_weights[section_number], step_bias)
        out_grad = ((hidden_state.astype(jnp.float32) - target[:, latent_index].astype(jnp.float32)) / LATENTS).astype(jnp.bfloat16)
        new_totals = list(totals)
        for section_number in reversed(range(SECTIONS)):
            weight_part, out_grad = backward_block(section_inputs[section_number], out_grad, section_weights[section_number], biases[section_number])
            new_totals[section_number] = totals[section_number] + weight_part
        return (tuple(new_totals), None)
    start_totals = tuple((jnp.zeros((C, 9, C), jnp.float32) for section_number in range(SECTIONS)))
    totals, unused = lax.scan(one_latent, start_totals, jnp.arange(LATENTS, dtype=jnp.int32))
    return jnp.stack(totals)
```

```python
import functools

import jax
import jax.numpy as jnp
from jax import lax
from jax.experimental import pallas as pl
from jax.experimental.pallas import tpu as pltpu
from jax.sharding import PartitionSpec as P

GROUP = 20
RES = 16
MOD = 65521
MESH = pl.DeviceIdType.MESH


def below_mod(value):
    value = (value >> 16) * 15 + (value & 65535)
    value = (value >> 16) * 15 + (value & 65535)
    return jnp.where(value >= MOD, value - MOD, value)


def group_sums(values_list, group):
    rows, lanes = values_list[0].shape
    groups = rows // group
    parts = []
    for values in values_list:
        while values.shape[1] > 128:
            half = values.shape[1] // 2
            values = values[:, :half] + values[:, half:]
        for g in range(groups):
            first, last = g * group, (g + 1) * group
            start, end = first // 8 * 8, -(-last // 8) * 8
            total = None
            for row in range(start, end, 8):
                tile = values[row : row + 8]
                if row < first or row + 8 > last:
                    place = lax.broadcasted_iota(jnp.int32, tile.shape, 0) + row
                    tile = jnp.where((place >= first) & (place < last), tile, 0.0)
                total = tile if total is None else total + tile
            parts.append(jnp.sum(total, axis=0, keepdims=True))
    sums = jnp.sum(jnp.concatenate(parts, axis=0), axis=1, keepdims=True)
    place = lax.broadcasted_iota(jnp.int32, (rows, 1), 0)
    spread = []
    for index in range(len(values_list)):
        base = index * groups
        result = jnp.broadcast_to(sums[base : base + 1], (rows, 1))
        for g in range(1, groups):
            result = jnp.where(place >= g * group, sums[base + g : base + g + 1], result)
        spread.append(result)
    return spread


def tap_masks(pixels):
    place = lax.broadcasted_iota(jnp.int32, (1, pixels), 1)
    row, col = place // RES, place % RES
    return {-1: (row >= 1, col >= 1), 0: (None, None), 1: (row < RES - 1, col < RES - 1)}


def moved(values, offset):
    pixels = values.shape[1]
    return values if offset % pixels == 0 else pltpu.roll(values, (-offset) % pixels, axis=1)


def kernel(
    sizes,
    latents_ref,
    target_ref,
    base_ref,
    seed_ref,
    steps_ref,
    table_ref,
    out_ref,
    weight,
    weight_t,
    bias,
    part_send,
    part_recv,
    shift_send,
    shift_recv,
    grad_send,
    grad_recv,
    columns,
    normed,
    scale,
    slope,
    held,
    total,
    sum_send,
    sum_recv,
    own_sum,
    part_sem,
    shift_sem,
    grad_sem,
    sum_sem,
    out_sem,
    send_sem,
):
    replicas, sections, shards, latents_here, all_latents = sizes
    dp = lax.axis_index("dp")
    section = lax.axis_index("section")
    shard = lax.axis_index("tensor")
    channels, pixels = held.shape
    wide = weight.shape[1]
    last = sections - 1
    piece = sum_recv.shape[1]
    owners = weight.shape[0] // piece

    barrier = pltpu.get_barrier_semaphore()

    def greet(section_to, skip_own):
        for j in range(1 if skip_own else 0, shards):
            pl.semaphore_signal(
                barrier,
                inc=1,
                device_id={"section": section_to, "tensor": lax.rem(shard + j, shards)},
                device_id_type=MESH,
            )

    @pl.when(section > 0)
    def _():
        greet(section - 1, False)

    @pl.when(section < last)
    def _():
        greet(section + 1, False)

    @pl.when(section == last)
    def _():
        greet(section, True)

    for j in range(1, replicas):
        pl.semaphore_signal(
            barrier, inc=1, device_id={"dp": lax.rem(dp + j, replicas)}, device_id_type=MESH
        )

    seed = seed_ref[0]
    out_channel = lax.broadcasted_iota(jnp.int32, (8, wide), 1)
    out_part = below_mod(out_channel[0:1] * 32749)
    row_channel = lax.broadcasted_iota(jnp.int32, (channels, 128), 0) + shard * channels
    lane = lax.broadcasted_iota(jnp.int32, (channels, 128), 1)
    for tap in range(9):
        first_index = (row_channel * 9 + tap) * wide
        high = first_index >> 16
        low = high * 15 + (first_index & 65535)
        over = low >= MOD
        low = jnp.where(over, low - MOD, low)
        high = jnp.where(over, high + 1, high)
        row_part = below_mod(low * 32749 + high * 12345 + seed)
        for col in range(0, wide, 128):
            size = min(128, wide - col)
            mixed = row_part[:, :size] + out_part[:, col : col + size]
            mixed = jnp.where(low[:, :size] + lane[:, :size] >= MOD - col, mixed + 12345, mixed)
            mixed = jnp.where(mixed >= MOD, mixed - MOD, mixed)
            mixed = jnp.where(mixed >= MOD, mixed - MOD, mixed)
            noise = mixed.astype(jnp.float32) / 65521.0 - 0.5
            weight[tap * channels : (tap + 1) * channels, col : col + size] = (
                base_ref[tap, :, col : col + size].astype(jnp.float32) + 0.02 * noise
            ).astype(jnp.bfloat16)
    weight_t[...] = weight[...].T

    table_step = lax.broadcasted_iota(jnp.int32, table_ref.shape, 1)
    table = table_ref[...].astype(jnp.float32)
    for latent in range(latents_here):
        bias[latent] = jnp.broadcast_to(
            jnp.sum(
                jnp.where(table_step == steps_ref[latent], table, 0.0), axis=1, keepdims=True
            ),
            (channels, 128),
        )

    @pl.when(section == 0)
    def _():
        pl.semaphore_wait(barrier, replicas - 1 + shards)

    @pl.when((section > 0) & (section < last))
    def _():
        pl.semaphore_wait(barrier, replicas - 1 + 2 * shards)

    @pl.when(section == last)
    def _():
        pl.semaphore_wait(barrier, replicas - 1 + 2 * shards - 1)

    masks = tap_masks(pixels)
    count = float(GROUP * pixels)

    def wait_for(ref, sem):
        pltpu.make_async_copy(ref, ref, sem).wait()

    def send(source, place, sent, arrived, device):
        pltpu.make_async_remote_copy(
            src_ref=source,
            dst_ref=place,
            send_sem=sent,
            recv_sem=arrived,
            device_id=device,
            device_id_type=MESH,
        ).start()

    order = [j for j in (4, 3, 5, 2, 6, 1, 7, 0) if j < shards]
    order += [j for j in range(shards) if j not in order]

    def send_parts(latent):
        @pl.when(section < last)
        def _():
            for j in order:
                peer = lax.rem(shard + j, shards)
                send(
                    part_send.at[latent, peer],
                    part_recv.at[0, latent, shard],
                    send_sem.at[0, latent],
                    part_sem.at[0, latent],
                    {"section": section + 1, "tensor": peer},
                )

        @pl.when(section == last)
        def _():
            for j in order:
                peer = lax.rem(shard + j, shards)
                if j:
                    send(
                        part_send.at[latent, peer],
                        part_recv.at[1, latent, shard],
                        send_sem.at[0, latent],
                        part_sem.at[1, latent],
                        {"tensor": peer},
                    )
                else:
                    pltpu.make_async_copy(
                        part_send.at[latent, shard],
                        part_recv.at[1, latent, shard],
                        part_sem.at[1, latent],
                    ).start()

    def summed(phase, latent, start):
        result = start
        for j in range(shards):
            result = result + part_recv[phase, latent, j].astype(jnp.float32)
        return result.astype(jnp.bfloat16)

    def forward(latent):
        @pl.when(section == 0)
        def _():
            held[...] = latents_ref[latent].astype(jnp.float32)

        @pl.when(section > 0)
        def _():
            wait_for(shift_recv.at[latent], shift_sem.at[latent])
            wait_for(part_recv.at[0, latent], part_sem.at[0, latent])
            held[...] = summed(0, latent, shift_recv[latent]).astype(jnp.float32)

        shifted = held[...] + bias[latent][:, 0:1]
        shift_send[latent] = shifted

        @pl.when(section < last)
        def _():
            send(
                shift_send.at[latent],
                shift_recv.at[latent],
                send_sem.at[2, latent],
                shift_sem.at[latent],
                {"section": section + 1},
            )

        (sums,) = group_sums([shifted], GROUP)
        center = shifted - sums / count
        (squares,) = group_sums([center * center], GROUP)
        factor = lax.rsqrt(squares / count + 1e-05)
        value = center * factor
        sigmoid = 1.0 / (1.0 + jnp.exp(-value))
        activation = (value * sigmoid).astype(jnp.bfloat16).astype(jnp.float32)
        for dj in (-1, 0, 1):
            across = moved(activation, dj)
            if dj:
                across = jnp.where(masks[dj][1], across, 0.0)
            for di in (-1, 0, 1):
                tap = (di + 1) * 3 + dj + 1
                both = moved(across, di * RES)
                if di:
                    both = jnp.where(masks[di][0], both, 0.0)
                columns[latent, tap * channels : (tap + 1) * channels] = both.astype(jnp.bfloat16)
        part_send[latent] = (
            jnp.dot(weight_t[...], columns[latent], preferred_element_type=jnp.float32)
            .astype(jnp.bfloat16)
            .reshape(shards, channels, pixels)
        )
        send_parts(latent)
        normed[latent] = value
        scale[latent] = jnp.broadcast_to(factor, (channels, 128))
        slope[latent] = sigmoid * (1.0 + value * (1.0 - sigmoid))

    for latent in range(latents_here):
        forward(latent)

    grad_back = grad_send.at[1]
    grad_first = grad_send.at[0]

    for latent in range(latents_here):

        @pl.when(section == last)
        def _(latent=latent):
            wait_for(part_recv.at[1, latent], part_sem.at[1, latent])
            output = summed(1, latent, shift_send[latent]).astype(jnp.float32)
            grad_first[latent] = (
                (output - target_ref[latent].astype(jnp.float32)) / float(all_latents)
            ).astype(jnp.bfloat16)
            for j in order:
                peer = lax.rem(shard + j, shards)
                if j:
                    send(
                        grad_first.at[latent],
                        grad_recv.at[latent, shard],
                        send_sem.at[3, latent],
                        grad_sem.at[latent],
                        {"tensor": peer},
                    )
                else:
                    pltpu.make_async_copy(
                        grad_first.at[latent], grad_recv.at[latent, shard], grad_sem.at[latent]
                    ).start()

        wait_for(grad_recv.at[latent], grad_sem.at[latent])
        out_grad = grad_recv[latent].reshape(wide, pixels)

        @pl.when(section > 0)
        def _(latent=latent, out_grad=out_grad):
            spread = jnp.dot(weight[...], out_grad, preferred_element_type=jnp.float32)
            col_grad = None
            for dj in (-1, 0, 1):
                down = None
                for di in (-1, 0, 1):
                    tap = (di + 1) * 3 + dj + 1
                    term = spread[tap * channels : (tap + 1) * channels]
                    if di:
                        term = moved(jnp.where(masks[di][0], term, 0.0), -di * RES)
                    down = term if down is None else down + term
                if dj:
                    down = moved(jnp.where(masks[dj][1], down, 0.0), -dj)
                col_grad = down if col_grad is None else col_grad + down
            value = normed[latent]
            inner = col_grad * slope[latent]
            mean_inner, mean_both = group_sums([inner, inner * value], GROUP)
            in_grad = scale[latent][:, 0:1] * (
                inner - mean_inner / count - value * (mean_both / count)
            )
            grad_back[latent] = (
                grad_recv[latent, shard].astype(jnp.float32) + in_grad
            ).astype(jnp.bfloat16)
            for j in order:
                send(
                    grad_back.at[latent],
                    grad_recv.at[latent, shard],
                    send_sem.at[1, latent],
                    grad_sem.at[latent],
                    {"section": section - 1, "tensor": lax.rem(shard + j, shards)},
                )

        part = lax.dot_general(
            columns[latent], out_grad, (((1,), (1,)), ((), ())), preferred_element_type=jnp.float32
        )
        if latent == 0 and latents_here > 1:
            total[...] = part
        elif latent < latents_here - 1:
            total[...] += part
        else:
            if latent:
                part = total[...] + part
            sum_send[...] = part.astype(jnp.bfloat16)

    for j in range(1, replicas + 1):
        owner = lax.rem(dp + j, replicas)
        rows = pl.ds(pl.multiple_of(owner * piece, 16), piece)

        @pl.when(owner < owners)
        def _(j=j, owner=owner, rows=rows):
            if j < replicas:
                send(
                    sum_send.at[rows], sum_recv.at[dp], send_sem.at[4, 0], sum_sem, {"dp": owner}
                )
            else:
                pltpu.make_async_copy(sum_send.at[rows], sum_recv.at[dp], sum_sem).start()

    @pl.when(dp < owners)
    def _():
        wait_for(sum_recv, sum_sem)
        result = sum_recv[0].astype(jnp.float32)
        for j in range(1, replicas):
            result = result + sum_recv[j].astype(jnp.float32)
        own_sum[...] = result.astype(jnp.bfloat16)
        rows = pl.ds(pl.multiple_of(dp * piece, 16), piece)
        for j in range(1, replicas + 1):
            if j < replicas:
                send(
                    own_sum,
                    out_ref.at[rows],
                    send_sem.at[4, 1],
                    out_sem,
                    {"dp": lax.rem(dp + j, replicas)},
                )
            else:
                pltpu.make_async_copy(own_sum, out_ref.at[rows], out_sem).start()

    for latent in range(latents_here):

        @pl.when(section < last)
        def _(latent=latent):
            wait_for(part_send.at[latent], send_sem.at[0, latent])
            wait_for(shift_send.at[latent], send_sem.at[2, latent])

        @pl.when(section == last)
        def _(latent=latent):
            others = part_send.at[latent, pl.ds(0, shards - 1)]
            wait_for(others, send_sem.at[0, latent])
            wait_for(others, send_sem.at[3, latent])

        @pl.when(section > 0)
        def _(latent=latent):
            wait_for(part_send.at[latent], send_sem.at[1, latent])

    @pl.when(dp < owners)
    def _():
        wait_for(sum_send.at[pl.ds(0, (owners - 1) * piece)], send_sem.at[4, 0])
        wait_for(sum_recv.at[pl.ds(0, replicas - 1)], send_sem.at[4, 1])

    @pl.when(dp >= owners)
    def _():
        wait_for(sum_send, send_sem.at[4, 0])

    wait_for(out_ref, out_sem)


def body(latents, target, base_weight, seeds, timesteps, time_table):
    replicas, sections, shards = (lax.axis_size(name) for name in ("dp", "section", "tensor"))
    channels, latents_here, pixels = latents.shape
    wide = base_weight.shape[3]
    rows = 9 * channels
    owners = max(n for n in range(1, replicas + 1) if (rows // 16) % n == 0)
    sizes = (replicas, sections, shards, latents_here, latents_here * replicas)
    vmem = pl.BlockSpec(memory_space=pltpu.VMEM)
    smem = pl.BlockSpec(memory_space=pltpu.SMEM)
    bf16, f32 = jnp.bfloat16, jnp.float32
    here = latents_here
    scratch = [
        pltpu.VMEM((rows, wide), bf16),
        pltpu.VMEM((wide, rows), bf16),
        pltpu.VMEM((here, channels, 128), f32),
        pltpu.VMEM((here, shards, channels, pixels), bf16),
        pltpu.VMEM((2, here, shards, channels, pixels), bf16),
        pltpu.VMEM((here, channels, pixels), f32),
        pltpu.VMEM((here, channels, pixels), f32),
        pltpu.VMEM((2, here, channels, pixels), bf16),
        pltpu.VMEM((here, shards, channels, pixels), bf16),
        pltpu.VMEM((here, rows, pixels), bf16),
        pltpu.VMEM((here, channels, pixels), f32),
        pltpu.VMEM((here, channels, 128), f32),
        pltpu.VMEM((here, channels, pixels), f32),
        pltpu.VMEM((channels, pixels), f32),
        pltpu.VMEM((rows, wide), f32),
        pltpu.VMEM((rows, wide), bf16),
        pltpu.VMEM((replicas, rows // owners, wide), bf16),
        pltpu.VMEM((rows // owners, wide), bf16),
        pltpu.SemaphoreType.DMA((2, here)),
        pltpu.SemaphoreType.DMA((here,)),
        pltpu.SemaphoreType.DMA((here,)),
        pltpu.SemaphoreType.DMA,
        pltpu.SemaphoreType.DMA,
        pltpu.SemaphoreType.DMA((5, 2)),
    ]
    result = pl.pallas_call(
        functools.partial(kernel, sizes),
        out_shape=jax.ShapeDtypeStruct((rows, wide), bf16),
        in_specs=[vmem, vmem, vmem, smem, smem, vmem],
        out_specs=vmem,
        scratch_shapes=scratch,
        compiler_params=pltpu.CompilerParams(
            collective_id=0, has_side_effects=True, vmem_limit_bytes=48 * 1024 * 1024
        ),
        cost_estimate=pl.CostEstimate(
            flops=6 * here * rows * wide * pixels, bytes_accessed=4 * rows * wide, transcendentals=0
        ),
    )(
        latents.transpose(1, 0, 2),
        target.transpose(1, 0, 2),
        base_weight[0].transpose(1, 0, 2),
        seeds,
        timesteps,
        time_table[0].T,
    )
    return result.astype(f32).reshape(9, channels, wide).transpose(1, 0, 2)[None]


def solution(mesh):
    in_specs = (
        P("tensor", "dp", None),
        P("tensor", "dp", None),
        P("section", "tensor", None, None),
        P("section"),
        P("dp"),
        P("section", None, "tensor"),
    )
    out_specs = P("section", "tensor", None, None)
    return jax.shard_map(body, mesh=mesh, in_specs=in_specs, out_specs=out_specs, check_vma=False)
```

```python
import functools

import jax
import jax.numpy as jnp
from jax import lax
from jax.experimental import pallas as pl
from jax.experimental.pallas import tpu as pltpu
from jax.sharding import PartitionSpec as P

GROUP = 20
RES = 16
MOD = 65521
CHUNK = 16
SIDE = 4
MESH = pl.DeviceIdType.MESH


def below_mod(value):
    value = (value >> 16) * 15 + (value & 65535)
    value = (value >> 16) * 15 + (value & 65535)
    return jnp.where(value >= MOD, value - MOD, value)


def group_sums(values_list, group):
    rows, lanes = values_list[0].shape
    groups = rows // group
    parts = []
    for values in values_list:
        while values.shape[1] > 128:
            half = values.shape[1] // 2
            values = values[:, :half] + values[:, half:]
        for g in range(groups):
            first, last = g * group, (g + 1) * group
            start, end = first // 8 * 8, -(-last // 8) * 8
            total = None
            for row in range(start, end, 8):
                tile = values[row : row + 8]
                if row < first or row + 8 > last:
                    place = lax.broadcasted_iota(jnp.int32, tile.shape, 0) + row
                    tile = jnp.where((place >= first) & (place < last), tile, 0.0)
                total = tile if total is None else total + tile
            parts.append(jnp.sum(total, axis=0, keepdims=True))
    sums = jnp.sum(jnp.concatenate(parts, axis=0), axis=1, keepdims=True)
    place = lax.broadcasted_iota(jnp.int32, (rows, 1), 0)
    spread = []
    for index in range(len(values_list)):
        base = index * groups
        result = jnp.broadcast_to(sums[base : base + 1], (rows, 1))
        for g in range(1, groups):
            result = jnp.where(place >= g * group, sums[base + g : base + g + 1], result)
        spread.append(result)
    return spread


def tap_masks(pixels):
    place = lax.broadcasted_iota(jnp.int32, (1, pixels), 1)
    row, col = place // RES, place % RES
    return {-1: (row >= 1, col >= 1), 0: (None, None), 1: (row < RES - 1, col < RES - 1)}


def moved(values, offset):
    pixels = values.shape[1]
    return values if offset % pixels == 0 else pltpu.roll(values, (-offset) % pixels, axis=1)


def kernel(
    sizes,
    latents_hbm,
    target_hbm,
    base_hbm,
    seed_ref,
    steps_ref,
    table_hbm,
    out_ref,
    latents_ref,
    target_ref,
    base_ref,
    table_ref,
    load_sem,
    weight,
    weight_t,
    bias,
    part_send,
    part_recv,
    shift_send,
    shift_recv,
    grad_send,
    grad_recv,
    columns,
    normed,
    scale,
    slope,
    held,
    total,
    sum_send,
    sum_recv,
    own_sum,
    across_recv,
    across_sum,
    part_sem,
    shift_sem,
    grad_sem,
    sum_sem,
    out_sem,
    send_sem,
):
    replicas, sections, shards, latents_here, all_latents = sizes
    dp = lax.axis_index("dp")
    section = lax.axis_index("section")
    shard = lax.axis_index("tensor")
    channels, pixels = held.shape
    wide = weight.shape[1]
    last = sections - 1
    piece = sum_recv.shape[1]
    chunks = [(start, min(CHUNK, piece - start)) for start in range(0, piece, CHUNK)]

    loads = [
        pltpu.make_async_copy(source, place, load_sem.at[n])
        for n, (source, place) in enumerate(
            [
                (base_hbm, base_ref),
                (table_hbm, table_ref),
                (latents_hbm, latents_ref),
                (target_hbm, target_ref),
            ]
        )
    ]
    for load in loads:
        load.start()

    barrier = pltpu.get_barrier_semaphore()

    def greet(section_to, skip_own):
        for j in range(1 if skip_own else 0, shards):
            pl.semaphore_signal(
                barrier,
                inc=1,
                device_id={"section": section_to, "tensor": lax.rem(shard + j, shards)},
                device_id_type=MESH,
            )

    @pl.when(section > 0)
    def _():
        greet(section - 1, False)

    @pl.when(section < last)
    def _():
        greet(section + 1, False)

    @pl.when(section == last)
    def _():
        greet(section, True)

    for j in range(1, replicas):
        pl.semaphore_signal(
            barrier, inc=1, device_id={"dp": lax.rem(dp + j, replicas)}, device_id_type=MESH
        )

    for load in loads:
        load.wait()

    seed = seed_ref[0]
    out_channel = lax.broadcasted_iota(jnp.int32, (8, wide), 1)
    out_part = below_mod(out_channel[0:1] * 32749)
    row_channel = lax.broadcasted_iota(jnp.int32, (channels, 128), 0) + shard * channels
    lane = lax.broadcasted_iota(jnp.int32, (channels, 128), 1)
    for tap in range(9):
        first_index = (row_channel * 9 + tap) * wide
        high = first_index >> 16
        low = high * 15 + (first_index & 65535)
        over = low >= MOD
        low = jnp.where(over, low - MOD, low)
        high = jnp.where(over, high + 1, high)
        row_part = below_mod(low * 32749 + high * 12345 + seed)
        for col in range(0, wide, 128):
            size = min(128, wide - col)
            mixed = row_part[:, :size] + out_part[:, col : col + size]
            mixed = jnp.where(low[:, :size] + lane[:, :size] >= MOD - col, mixed + 12345, mixed)
            mixed = jnp.where(mixed >= MOD, mixed - MOD, mixed)
            mixed = jnp.where(mixed >= MOD, mixed - MOD, mixed)
            noise = mixed.astype(jnp.float32) / 65521.0 - 0.5
            weight[tap * channels : (tap + 1) * channels, col : col + size] = (
                base_ref[tap, :, col : col + size].astype(jnp.float32) + 0.02 * noise
            ).astype(jnp.bfloat16)
    weight_t[...] = weight[...].T

    table_step = lax.broadcasted_iota(jnp.int32, table_ref.shape, 1)
    table = table_ref[...].astype(jnp.float32)
    for latent in range(latents_here):
        bias[latent] = jnp.broadcast_to(
            jnp.sum(
                jnp.where(table_step == steps_ref[latent], table, 0.0), axis=1, keepdims=True
            ),
            (channels, 128),
        )

    @pl.when(section == 0)
    def _():
        pl.semaphore_wait(barrier, replicas - 1 + shards)

    @pl.when((section > 0) & (section < last))
    def _():
        pl.semaphore_wait(barrier, replicas - 1 + 2 * shards)

    @pl.when(section == last)
    def _():
        pl.semaphore_wait(barrier, replicas - 1 + 2 * shards - 1)

    masks = tap_masks(pixels)
    count = float(GROUP * pixels)

    def wait_for(ref, sem):
        pltpu.make_async_copy(ref, ref, sem).wait()

    def send(source, place, sent, arrived, device):
        pltpu.make_async_remote_copy(
            src_ref=source,
            dst_ref=place,
            send_sem=sent,
            recv_sem=arrived,
            device_id=device,
            device_id_type=MESH,
        ).start()

    order = [j for j in (4, 3, 5, 2, 6, 1, 7, 0) if j < shards]
    order += [j for j in range(shards) if j not in order]

    def send_parts(latent):
        @pl.when(section < last)
        def _():
            for j in order:
                peer = lax.rem(shard + j, shards)
                send(
                    part_send.at[latent, peer],
                    part_recv.at[0, latent, shard],
                    send_sem.at[0, latent],
                    part_sem.at[0, latent],
                    {"section": section + 1, "tensor": peer},
                )

        @pl.when(section == last)
        def _():
            for j in order:
                peer = lax.rem(shard + j, shards)
                if j:
                    send(
                        part_send.at[latent, peer],
                        part_recv.at[1, latent, shard],
                        send_sem.at[0, latent],
                        part_sem.at[1, latent],
                        {"tensor": peer},
                    )
                else:
                    pltpu.make_async_copy(
                        part_send.at[latent, shard],
                        part_recv.at[1, latent, shard],
                        part_sem.at[1, latent],
                    ).start()

    def summed(phase, latent, start):
        result = start
        for j in range(shards):
            result = result + part_recv[phase, latent, j].astype(jnp.float32)
        return result.astype(jnp.bfloat16)

    def forward(latent):
        @pl.when(section == 0)
        def _():
            held[...] = latents_ref[latent].astype(jnp.float32)

        @pl.when(section > 0)
        def _():
            wait_for(shift_recv.at[latent], shift_sem.at[latent])
            wait_for(part_recv.at[0, latent], part_sem.at[0, latent])
            held[...] = summed(0, latent, shift_recv[latent]).astype(jnp.float32)

        shifted = held[...] + bias[latent][:, 0:1]
        shift_send[latent] = shifted

        @pl.when(section < last)
        def _():
            send(
                shift_send.at[latent],
                shift_recv.at[latent],
                send_sem.at[2, latent],
                shift_sem.at[latent],
                {"section": section + 1},
            )

        (sums,) = group_sums([shifted], GROUP)
        center = shifted - sums / count
        (squares,) = group_sums([center * center], GROUP)
        factor = lax.rsqrt(squares / count + 1e-05)
        value = center * factor
        sigmoid = 1.0 / (1.0 + jnp.exp(-value))
        activation = (value * sigmoid).astype(jnp.bfloat16).astype(jnp.float32)
        for dj in (-1, 0, 1):
            across = moved(activation, dj)
            if dj:
                across = jnp.where(masks[dj][1], across, 0.0)
            for di in (-1, 0, 1):
                tap = (di + 1) * 3 + dj + 1
                both = moved(across, di * RES)
                if di:
                    both = jnp.where(masks[di][0], both, 0.0)
                columns[latent, tap * channels : (tap + 1) * channels] = both.astype(jnp.bfloat16)
        part_send[latent] = (
            jnp.dot(weight_t[...], columns[latent], preferred_element_type=jnp.float32)
            .astype(jnp.bfloat16)
            .reshape(shards, channels, pixels)
        )
        send_parts(latent)
        normed[latent] = value
        scale[latent] = jnp.broadcast_to(factor, (channels, 128))
        slope[latent] = sigmoid * (1.0 + value * (1.0 - sigmoid))

    for latent in range(latents_here):
        forward(latent)

    grad_back = grad_send.at[1]
    grad_first = grad_send.at[0]

    for latent in range(latents_here):

        @pl.when(section == last)
        def _(latent=latent):
            wait_for(part_recv.at[1, latent], part_sem.at[1, latent])
            output = summed(1, latent, shift_send[latent]).astype(jnp.float32)
            grad_first[latent] = (
                (output - target_ref[latent].astype(jnp.float32)) / float(all_latents)
            ).astype(jnp.bfloat16)
            for j in order:
                peer = lax.rem(shard + j, shards)
                if j:
                    send(
                        grad_first.at[latent],
                        grad_recv.at[latent, shard],
                        send_sem.at[3, latent],
                        grad_sem.at[latent],
                        {"tensor": peer},
                    )
                else:
                    pltpu.make_async_copy(
                        grad_first.at[latent], grad_recv.at[latent, shard], grad_sem.at[latent]
                    ).start()

    for latent in range(latents_here):
        wait_for(grad_recv.at[latent], grad_sem.at[latent])
        out_grad = grad_recv[latent].reshape(wide, pixels)

        @pl.when(section > 0)
        def _(latent=latent, out_grad=out_grad):
            spread = jnp.dot(weight[...], out_grad, preferred_element_type=jnp.float32)
            col_grad = None
            for dj in (-1, 0, 1):
                down = None
                for di in (-1, 0, 1):
                    tap = (di + 1) * 3 + dj + 1
                    term = spread[tap * channels : (tap + 1) * channels]
                    if di:
                        term = moved(jnp.where(masks[di][0], term, 0.0), -di * RES)
                    down = term if down is None else down + term
                if dj:
                    down = moved(jnp.where(masks[dj][1], down, 0.0), -dj)
                col_grad = down if col_grad is None else col_grad + down
            value = normed[latent]
            inner = col_grad * slope[latent]
            mean_inner, mean_both = group_sums([inner, inner * value], GROUP)
            in_grad = scale[latent][:, 0:1] * (
                inner - mean_inner / count - value * (mean_both / count)
            )
            grad_back[latent] = (
                grad_recv[latent, shard].astype(jnp.float32) + in_grad
            ).astype(jnp.bfloat16)
            for j in order:
                send(
                    grad_back.at[latent],
                    grad_recv.at[latent, shard],
                    send_sem.at[1, latent],
                    grad_sem.at[latent],
                    {"section": section - 1, "tensor": lax.rem(shard + j, shards)},
                )

        part = lax.dot_general(
            columns[latent], out_grad, (((1,), (1,)), ((), ())), preferred_element_type=jnp.float32
        )
        if latent == 0 and latents_here > 1:
            total[...] = part
        elif latent < latents_here - 1:
            total[...] += part
        else:
            if latent:
                part = total[...] + part
            rows = part.shape[0]
            sum_send[:rows] = part.astype(jnp.bfloat16)
            if rows < sum_send.shape[0]:
                sum_send[rows:] = jnp.zeros((sum_send.shape[0] - rows, wide), jnp.bfloat16)

    def added(ref, rows):
        result = ref[0, rows].astype(jnp.float32)
        for j in range(1, ref.shape[0]):
            result = result + ref[j, rows].astype(jnp.float32)
        return result.astype(jnp.bfloat16)

    def part_rows(start, size):
        return pl.ds(pl.multiple_of(start, 16), size)

    @pl.when(section == 0)
    def _():
        for c, (start, size) in enumerate(chunks):
            for j in range(1, replicas + 1):
                owner = lax.rem(dp + j, replicas)
                source = sum_send.at[part_rows(owner * piece + start, size)]
                place = sum_recv.at[dp, pl.ds(start, size)]
                if j < replicas:
                    send(source, place, send_sem.at[4, 0], sum_sem.at[c], {"dp": owner})
                else:
                    pltpu.make_async_copy(source, place, sum_sem.at[c]).start()
        for c, (start, size) in enumerate(chunks):
            rows = pl.ds(start, size)
            wait_for(sum_recv.at[:, rows], sum_sem.at[c])
            own_sum[rows] = added(sum_recv, rows)
            place = out_ref.at[part_rows(dp * piece + start, size)]
            for j in range(1, replicas + 1):
                if j < replicas:
                    other = {"dp": lax.rem(dp + j, replicas)}
                    send(own_sum.at[rows], place, send_sem.at[4, 1], out_sem.at[0], other)
                else:
                    pltpu.make_async_copy(own_sum.at[rows], place, out_sem.at[0]).start()
        wait_for(out_ref, out_sem.at[0])
        wait_for(sum_recv.at[pl.ds(0, replicas - 1)], send_sem.at[4, 0])
        wait_for(sum_recv.at[pl.ds(0, replicas - 1)], send_sem.at[4, 1])

    @pl.when(section > 0)
    def _():
        side = across_recv.shape[0]
        other_side = replicas // side
        strip = piece * other_side
        x, y = dp // other_side, lax.rem(dp, other_side)
        for j in range(1, side + 1):
            to = lax.rem(x + j, side)
            source, place = sum_send.at[part_rows(to * strip, strip)], across_recv.at[x]
            if j < side:
                device = {"dp": to * other_side + y}
                send(source, place, send_sem.at[4, 0], sum_sem.at[0], device)
            else:
                pltpu.make_async_copy(source, place, sum_sem.at[0]).start()
        wait_for(across_recv, sum_sem.at[0])
        across_sum[...] = added(across_recv, pl.ds(0, strip))
        for j in range(1, other_side + 1):
            to = lax.rem(y + j, other_side)
            source, place = across_sum.at[part_rows(to * piece, piece)], sum_recv.at[y]
            if j < other_side:
                device = {"dp": x * other_side + to}
                send(source, place, send_sem.at[4, 1], sum_sem.at[1], device)
            else:
                pltpu.make_async_copy(source, place, sum_sem.at[1]).start()
        wait_for(sum_recv.at[pl.ds(0, other_side)], sum_sem.at[1])
        own_sum[...] = added(sum_recv.at[pl.ds(0, other_side)], pl.ds(0, piece))
        place = out_ref.at[part_rows(dp * piece, piece)]
        for j in range(1, other_side + 1):
            if j < other_side:
                device = {"dp": x * other_side + lax.rem(y + j, other_side)}
                send(own_sum, place, send_sem.at[5, 0], out_sem.at[0], device)
            else:
                pltpu.make_async_copy(own_sum, place, out_sem.at[0]).start()
        mine = out_ref.at[part_rows(x * strip, strip)]
        wait_for(mine, out_sem.at[0])
        for j in range(1, side):
            device = {"dp": lax.rem(x + j, side) * other_side + y}
            send(mine, mine, send_sem.at[5, 1], out_sem.at[1], device)
        wait_for(across_recv.at[pl.ds(0, side - 1)], out_sem.at[1])
        wait_for(across_recv.at[pl.ds(0, side - 1)], send_sem.at[4, 0])
        wait_for(across_recv.at[pl.ds(0, side - 1)], send_sem.at[5, 1])
        wait_for(sum_recv.at[pl.ds(0, other_side - 1)], send_sem.at[4, 1])
        wait_for(sum_recv.at[pl.ds(0, other_side - 1)], send_sem.at[5, 0])

    for latent in range(latents_here):

        @pl.when(section < last)
        def _(latent=latent):
            wait_for(part_send.at[latent], send_sem.at[0, latent])
            wait_for(shift_send.at[latent], send_sem.at[2, latent])

        @pl.when(section == last)
        def _(latent=latent):
            others = part_send.at[latent, pl.ds(0, shards - 1)]
            wait_for(others, send_sem.at[0, latent])
            wait_for(others, send_sem.at[3, latent])

        @pl.when(section > 0)
        def _(latent=latent):
            wait_for(part_send.at[latent], send_sem.at[1, latent])


def body(latents, target, base_weight, seeds, timesteps, time_table):
    replicas, sections, shards = (lax.axis_size(name) for name in ("dp", "section", "tensor"))
    channels, latents_here, pixels = latents.shape
    wide = base_weight.shape[3]
    rows = 9 * channels
    piece = -(-rows // (16 * replicas)) * 16
    side = min(SIDE, replicas)
    strip = piece * (replicas // side)
    sizes = (replicas, sections, shards, latents_here, latents_here * replicas)
    vmem = pl.BlockSpec(memory_space=pltpu.VMEM)
    smem = pl.BlockSpec(memory_space=pltpu.SMEM)
    hbm = pl.BlockSpec(memory_space=pl.ANY)
    bf16, f32 = jnp.bfloat16, jnp.float32
    here = latents_here
    scratch = [
        pltpu.VMEM((here, channels, pixels), bf16),
        pltpu.VMEM((here, channels, pixels), bf16),
        pltpu.VMEM((9, channels, wide), bf16),
        pltpu.VMEM(time_table.shape[:0:-1], bf16),
        pltpu.SemaphoreType.DMA((4,)),
        pltpu.VMEM((rows, wide), bf16),
        pltpu.VMEM((wide, rows), bf16),
        pltpu.VMEM((here, channels, 128), f32),
        pltpu.VMEM((here, shards, channels, pixels), bf16),
        pltpu.VMEM((2, here, shards, channels, pixels), bf16),
        pltpu.VMEM((here, channels, pixels), f32),
        pltpu.VMEM((here, channels, pixels), f32),
        pltpu.VMEM((2, here, channels, pixels), bf16),
        pltpu.VMEM((here, shards, channels, pixels), bf16),
        pltpu.VMEM((here, rows, pixels), bf16),
        pltpu.VMEM((here, channels, pixels), f32),
        pltpu.VMEM((here, channels, 128), f32),
        pltpu.VMEM((here, channels, pixels), f32),
        pltpu.VMEM((channels, pixels), f32),
        pltpu.VMEM((rows, wide), f32),
        pltpu.VMEM((replicas * piece, wide), bf16),
        pltpu.VMEM((replicas, piece, wide), bf16),
        pltpu.VMEM((piece, wide), bf16),
        pltpu.VMEM((side, strip, wide), bf16),
        pltpu.VMEM((strip, wide), bf16),
        pltpu.SemaphoreType.DMA((2, here)),
        pltpu.SemaphoreType.DMA((here,)),
        pltpu.SemaphoreType.DMA((here,)),
        pltpu.SemaphoreType.DMA((max(2, -(-piece // CHUNK)),)),
        pltpu.SemaphoreType.DMA((2,)),
        pltpu.SemaphoreType.DMA((6, 2)),
    ]
    result = pl.pallas_call(
        functools.partial(kernel, sizes),
        out_shape=jax.ShapeDtypeStruct((replicas * piece, wide), bf16),
        in_specs=[hbm, hbm, hbm, smem, smem, hbm],
        out_specs=vmem,
        scratch_shapes=scratch,
        compiler_params=pltpu.CompilerParams(
            collective_id=0, has_side_effects=True, vmem_limit_bytes=48 * 1024 * 1024
        ),
        cost_estimate=pl.CostEstimate(
            flops=6 * here * rows * wide * pixels, bytes_accessed=4 * rows * wide, transcendentals=0
        ),
    )(
        latents.transpose(1, 0, 2),
        target.transpose(1, 0, 2),
        base_weight[0].transpose(1, 0, 2),
        seeds,
        timesteps,
        time_table[0].T,
    )
    return result[:rows].astype(f32).reshape(9, channels, wide).transpose(1, 0, 2)[None]


def solution(mesh):
    in_specs = (
        P("tensor", "dp", None),
        P("tensor", "dp", None),
        P("section", "tensor", None, None),
        P("section"),
        P("dp"),
        P("section", None, "tensor"),
    )
    out_specs = P("section", "tensor", None, None)
    return jax.shard_map(body, mesh=mesh, in_specs=in_specs, out_specs=out_specs, check_vma=False)
```

```python
import functools

import jax
import jax.numpy as jnp
from jax import lax
from jax.experimental import pallas as pl
from jax.experimental.pallas import tpu as pltpu
from jax.sharding import PartitionSpec as P

GROUP = 20
RES = 16
MOD = 65521
PIECES = (32, 16)
SIDE = 4
MESH = pl.DeviceIdType.MESH


def below_mod(value):
    value = (value >> 16) * 15 + (value & 65535)
    value = (value >> 16) * 15 + (value & 65535)
    return jnp.where(value >= MOD, value - MOD, value)


def group_sums(values_list, group):
    rows, lanes = values_list[0].shape
    groups = rows // group
    parts = []
    for values in values_list:
        while values.shape[1] > 128:
            half = values.shape[1] // 2
            values = values[:, :half] + values[:, half:]
        for g in range(groups):
            first, last = g * group, (g + 1) * group
            start, end = first // 8 * 8, -(-last // 8) * 8
            total = None
            for row in range(start, end, 8):
                tile = values[row : row + 8]
                if row < first or row + 8 > last:
                    place = lax.broadcasted_iota(jnp.int32, tile.shape, 0) + row
                    tile = jnp.where((place >= first) & (place < last), tile, 0.0)
                total = tile if total is None else total + tile
            parts.append(jnp.sum(total, axis=0, keepdims=True))
    sums = jnp.sum(jnp.concatenate(parts, axis=0), axis=1, keepdims=True)
    place = lax.broadcasted_iota(jnp.int32, (rows, 1), 0)
    spread = []
    for index in range(len(values_list)):
        base = index * groups
        result = jnp.broadcast_to(sums[base : base + 1], (rows, 1))
        for g in range(1, groups):
            result = jnp.where(place >= g * group, sums[base + g : base + g + 1], result)
        spread.append(result)
    return spread


def tap_masks(pixels):
    place = lax.broadcasted_iota(jnp.int32, (1, pixels), 1)
    row, col = place // RES, place % RES
    return {-1: (row >= 1, col >= 1), 0: (None, None), 1: (row < RES - 1, col < RES - 1)}


def moved(values, offset):
    pixels = values.shape[1]
    return values if offset % pixels == 0 else pltpu.roll(values, (-offset) % pixels, axis=1)


def kernel(
    sizes,
    latents_hbm,
    target_hbm,
    base_hbm,
    seed_hbm,
    steps_hbm,
    table_hbm,
    out_ref,
    latents_ref,
    target_ref,
    base_ref,
    table_ref,
    seed_ref,
    steps_ref,
    load_sem,
    weight,
    weight_t,
    bias,
    part_send,
    part_recv,
    shift_send,
    shift_recv,
    grad_send,
    grad_recv,
    columns,
    normed,
    scale,
    slope,
    held,
    total,
    sum_send,
    sum_recv,
    own_sum,
    across_recv,
    across_sum,
    sum_done,
    down_sem,
    up_sem,
    part_sem,
    shift_sem,
    grad_sem,
    sum_sem,
    out_sem,
    send_sem,
):
    replicas, sections, shards, latents_here, all_latents = sizes
    dp = lax.axis_index("dp")
    section = lax.axis_index("section")
    shard = lax.axis_index("tensor")
    channels, pixels = held.shape
    wide = weight.shape[1]
    last = sections - 1
    side = across_recv.shape[0]
    other_side = replicas // side
    x, y = dp // other_side, lax.rem(dp, other_side)
    chunks, start = [], 0
    for piece in PIECES:
        chunks.append((start, piece))
        start += piece * replicas

    loads = [
        pltpu.make_async_copy(source, place, load_sem.at[n])
        for n, (source, place) in enumerate(
            [
                (steps_hbm, steps_ref),
                (seed_hbm, seed_ref),
                (table_hbm, table_ref),
                (latents_hbm, latents_ref),
                (base_hbm, base_ref),
                (target_hbm, target_ref),
            ]
        )
    ]
    for load in loads:
        load.start()

    barrier = pltpu.get_barrier_semaphore()

    def greet(section_to, skip_own):
        for j in range(1 if skip_own else 0, shards):
            peer = lax.rem(shard + j, shards)
            pl.semaphore_signal(
                barrier,
                inc=1,
                device_id={"section": section_to, "tensor": peer},
                device_id_type=MESH,
            )

    @pl.when(section > 0)
    def _():
        greet(section - 1, False)

    @pl.when(section < last)
    def _():
        greet(section + 1, False)

    @pl.when(section == last)
    def _():
        greet(section, True)

    for j in range(1, replicas):
        pl.semaphore_signal(
            barrier, inc=1, device_id={"dp": lax.rem(dp + j, replicas)}, device_id_type=MESH
        )

    masks = tap_masks(pixels)
    count = float(GROUP * pixels)

    def wait_for(ref, sem):
        pltpu.make_async_copy(ref, ref, sem).wait()

    def send(source, place, sent, arrived, device):
        pltpu.make_async_remote_copy(
            src_ref=source,
            dst_ref=place,
            send_sem=sent,
            recv_sem=arrived,
            device_id=device,
            device_id_type=MESH,
        ).start()

    order = [j for j in (4, 3, 5, 2, 6, 1, 7, 0) if j < shards]
    order += [j for j in range(shards) if j not in order]

    def send_parts(latent):
        @pl.when(section < last)
        def _():
            for j in order:
                peer = lax.rem(shard + j, shards)
                send(
                    part_send.at[latent, peer],
                    part_recv.at[0, latent, shard],
                    send_sem.at[0, latent],
                    part_sem.at[0, latent],
                    {"section": section + 1, "tensor": peer},
                )

        @pl.when(section == last)
        def _():
            for j in order:
                peer = lax.rem(shard + j, shards)
                if j:
                    send(
                        part_send.at[latent, peer],
                        part_recv.at[1, latent, shard],
                        send_sem.at[0, latent],
                        part_sem.at[1, latent],
                        {"tensor": peer},
                    )
                else:
                    pltpu.make_async_copy(
                        part_send.at[latent, shard],
                        part_recv.at[1, latent, shard],
                        part_sem.at[1, latent],
                    ).start()

    def summed(phase, latent, start):
        result = start
        for j in range(shards):
            result = result + part_recv[phase, latent, j].astype(jnp.float32)
        return result.astype(jnp.bfloat16)

    def take(latent):
        @pl.when(section == 0)
        def _():
            held[...] = latents_ref[latent].astype(jnp.float32)

        @pl.when(section > 0)
        def _():
            wait_for(shift_recv.at[latent], shift_sem.at[latent])
            wait_for(part_recv.at[0, latent], part_sem.at[0, latent])
            held[...] = summed(0, latent, shift_recv[latent]).astype(jnp.float32)

        shift_send[latent] = held[...] + bias[latent][:, 0:1]

    def send_shift(latent):
        @pl.when(section < last)
        def _():
            send(
                shift_send.at[latent],
                shift_recv.at[latent],
                send_sem.at[2, latent],
                shift_sem.at[latent],
                {"section": section + 1},
            )

    def activate(latent):
        shifted = shift_send[latent]
        (sums,) = group_sums([shifted], GROUP)
        center = shifted - sums / count
        (squares,) = group_sums([center * center], GROUP)
        factor = lax.rsqrt(squares / count + 1e-05)
        value = center * factor
        sigmoid = 1.0 / (1.0 + jnp.exp(-value))
        activation = (value * sigmoid).astype(jnp.bfloat16).astype(jnp.float32)
        for dj in (-1, 0, 1):
            across = moved(activation, dj)
            if dj:
                across = jnp.where(masks[dj][1], across, 0.0)
            for di in (-1, 0, 1):
                tap = (di + 1) * 3 + dj + 1
                both = moved(across, di * RES)
                if di:
                    both = jnp.where(masks[di][0], both, 0.0)
                columns[latent, tap * channels : (tap + 1) * channels] = both.astype(jnp.bfloat16)
        normed[latent] = value
        slope[latent] = sigmoid
        scale[latent] = jnp.broadcast_to(factor, (channels, 128))

    def emit(latent):
        part_send[latent] = (
            jnp.dot(weight_t[...], columns[latent], preferred_element_type=jnp.float32)
            .astype(jnp.bfloat16)
            .reshape(shards, channels, pixels)
        )
        send_parts(latent)
        sigmoid = slope[latent]
        slope[latent] = sigmoid * (1.0 + normed[latent] * (1.0 - sigmoid))

    loads[0].wait()
    loads[2].wait()
    loads[3].wait()
    table_step = lax.broadcasted_iota(jnp.int32, table_ref.shape, 1)
    table = table_ref[...].astype(jnp.float32)
    for latent in range(latents_here):
        picked = jnp.where(table_step == steps_ref[latent], table, 0.0)
        own_bias = jnp.broadcast_to(jnp.sum(picked, axis=1, keepdims=True), (channels, 128))
        bias[latent] = own_bias

    @pl.when(section == 0)
    def _():
        take(0)
        activate(0)

    for n in (1, 4, 5):
        loads[n].wait()
    seed = seed_ref[0]
    out_channel = lax.broadcasted_iota(jnp.int32, (8, wide), 1)
    out_part = below_mod(out_channel[0:1] * 32749)
    row_channel = lax.broadcasted_iota(jnp.int32, (channels, 128), 0) + shard * channels
    lane = lax.broadcasted_iota(jnp.int32, (channels, 128), 1)
    for tap in range(9):
        first_index = (row_channel * 9 + tap) * wide
        high = first_index >> 16
        low = high * 15 + (first_index & 65535)
        over = low >= MOD
        low = jnp.where(over, low - MOD, low)
        high = jnp.where(over, high + 1, high)
        row_part = below_mod(low * 32749 + high * 12345 + seed)
        for col in range(0, wide, 128):
            size = min(128, wide - col)
            mixed = row_part[:, :size] + out_part[:, col : col + size]
            mixed = jnp.where(low[:, :size] + lane[:, :size] >= MOD - col, mixed + 12345, mixed)
            mixed = jnp.where(mixed >= MOD, mixed - MOD, mixed)
            mixed = jnp.where(mixed >= MOD, mixed - MOD, mixed)
            noise = mixed.astype(jnp.float32) / 65521.0 - 0.5
            weight[tap * channels : (tap + 1) * channels, col : col + size] = (
                base_ref[tap, :, col : col + size].astype(jnp.float32) + 0.02 * noise
            ).astype(jnp.bfloat16)
    weight_t[...] = weight[...].T

    for s in range(sections):
        amount = replicas - 1 + shards * ((s > 0) + (s < last)) + (shards - 1) * (s == last)

        @pl.when(section == s)
        def _(amount=amount):
            pl.semaphore_wait(barrier, amount)

    @pl.when(section > 0)
    def _():
        take(0)
        send_shift(0)
        activate(0)

    @pl.when(section == 0)
    def _():
        send_shift(0)

    emit(0)
    for latent in range(1, latents_here):
        take(latent)
        send_shift(latent)
        activate(latent)
        emit(latent)

    grad_back = grad_send.at[1]
    grad_first = grad_send.at[0]

    for latent in range(latents_here):

        @pl.when(section == last)
        def _(latent=latent):
            wait_for(part_recv.at[1, latent], part_sem.at[1, latent])
            output = summed(1, latent, shift_send[latent]).astype(jnp.float32)
            grad_first[latent] = (
                (output - target_ref[latent].astype(jnp.float32)) / float(all_latents)
            ).astype(jnp.bfloat16)
            for j in order:
                peer = lax.rem(shard + j, shards)
                if j:
                    send(
                        grad_first.at[latent],
                        grad_recv.at[latent, shard],
                        send_sem.at[3, latent],
                        grad_sem.at[latent],
                        {"tensor": peer},
                    )
                else:
                    pltpu.make_async_copy(
                        grad_first.at[latent], grad_recv.at[latent, shard], grad_sem.at[latent]
                    ).start()

    for latent in range(latents_here):
        wait_for(grad_recv.at[latent], grad_sem.at[latent])
        out_grad = grad_recv[latent].reshape(wide, pixels)

        @pl.when(section > 0)
        def _(latent=latent, out_grad=out_grad):
            spread = jnp.dot(weight[...], out_grad, preferred_element_type=jnp.float32)
            col_grad = None
            for dj in (-1, 0, 1):
                down = None
                for di in (-1, 0, 1):
                    tap = (di + 1) * 3 + dj + 1
                    term = spread[tap * channels : (tap + 1) * channels]
                    if di:
                        term = moved(jnp.where(masks[di][0], term, 0.0), -di * RES)
                    down = term if down is None else down + term
                if dj:
                    down = moved(jnp.where(masks[dj][1], down, 0.0), -dj)
                col_grad = down if col_grad is None else col_grad + down
            value = normed[latent]
            inner = col_grad * slope[latent]
            mean_inner, mean_both = group_sums([inner, inner * value], GROUP)
            in_grad = scale[latent][:, 0:1] * (
                inner - mean_inner / count - value * (mean_both / count)
            )
            grad_back[latent] = (
                grad_recv[latent, shard].astype(jnp.float32) + in_grad
            ).astype(jnp.bfloat16)
            for j in order:
                send(
                    grad_back.at[latent],
                    grad_recv.at[latent, shard],
                    send_sem.at[1, latent],
                    grad_sem.at[latent],
                    {
                        "section": section - 1,
                        "tensor": lax.rem(shard + j, shards),
                    },
                )

        part = lax.dot_general(
            columns[latent], out_grad, (((1,), (1,)), ((), ())), preferred_element_type=jnp.float32
        )
        if latent == 0 and latents_here > 1:
            total[...] = part
        elif latent < latents_here - 1:
            total[...] += part
        else:
            if latent:
                part = total[...] + part
            rows = part.shape[0]
            sum_send[:rows] = part.astype(jnp.bfloat16)
            if rows < sum_send.shape[0]:
                sum_send[rows:] = jnp.zeros((sum_send.shape[0] - rows, wide), jnp.bfloat16)

    def added(ref, rows):
        result = ref[0, rows].astype(jnp.float32)
        for j in range(1, ref.shape[0]):
            result = result + ref[j, rows].astype(jnp.float32)
        return result.astype(jnp.bfloat16)

    def place_of(c, x_to, y_to, strip=False):
        start, piece = chunks[c]
        row = start + (x_to * other_side + y_to) * piece
        return pl.ds(pl.multiple_of(row, 16), piece * (other_side if strip else 1))

    def kept(c, strip=False):
        start, piece = chunks[c]
        scale_by = side if strip else replicas
        return pl.ds(start // scale_by, piece * (other_side if strip else 1))

    @pl.when(section == 0)
    def _():
        for c in range(len(chunks)):
            for j in range(1, replicas + 1):
                owner = lax.rem(dp + j, replicas)
                source = sum_send.at[place_of(c, 0, owner)]
                place = sum_recv.at[dp, kept(c)]
                if j < replicas:
                    send(source, place, send_sem.at[4, 0], sum_sem.at[c], {"dp": owner})
                else:
                    pltpu.make_async_copy(source, place, sum_sem.at[c]).start()
        for c in range(len(chunks)):
            rows = kept(c)
            wait_for(sum_recv.at[:, rows], sum_sem.at[c])
            own_sum[rows] = added(sum_recv, rows)
            place = sum_done.at[place_of(c, 0, dp)]
            for j in range(1, replicas + 1):
                if j < replicas:
                    other = {"dp": lax.rem(dp + j, replicas)}
                    send(own_sum.at[rows], place, send_sem.at[4, 1], out_sem.at[0], other)
                else:
                    pltpu.make_async_copy(own_sum.at[rows], place, out_sem.at[0]).start()
        wait_for(sum_done, out_sem.at[0])
        wait_for(sum_recv.at[pl.ds(0, replicas - 1)], send_sem.at[4, 0])
        wait_for(sum_recv.at[pl.ds(0, replicas - 1)], send_sem.at[4, 1])

    @pl.when(section > 0)
    def _():
        def along_x(c):
            for j in range(1, side + 1):
                to = lax.rem(x + j, side)
                source = sum_send.at[place_of(c, to, 0, True)]
                place = across_recv.at[x, kept(c, True)]
                if j < side:
                    device = {"dp": to * other_side + y}
                    send(source, place, send_sem.at[4, 0], sum_sem.at[c], device)
                else:
                    pltpu.make_async_copy(source, place, sum_sem.at[c]).start()

        def along_y(c):
            start, piece = chunks[c]
            rows = kept(c, True)
            wait_for(across_recv.at[:, rows], sum_sem.at[c])
            across_sum[rows] = added(across_recv, rows)
            for j in range(1, other_side + 1):
                to = lax.rem(y + j, other_side)
                row = pl.multiple_of(start // side + to * piece, 16)
                source = across_sum.at[pl.ds(row, piece)]
                place = sum_recv.at[y, kept(c)]
                if j < other_side:
                    device = {"dp": x * other_side + to}
                    send(source, place, send_sem.at[4, 1], down_sem.at[c], device)
                else:
                    pltpu.make_async_copy(source, place, down_sem.at[c]).start()

        def back_y(c):
            rows = kept(c)
            wait_for(sum_recv.at[pl.ds(0, other_side), rows], down_sem.at[c])
            own_sum[rows] = added(sum_recv.at[pl.ds(0, other_side)], rows)
            place = sum_done.at[place_of(c, x, y)]
            for j in range(1, other_side + 1):
                if j < other_side:
                    device = {"dp": x * other_side + lax.rem(y + j, other_side)}
                    send(own_sum.at[rows], place, send_sem.at[5, 0], up_sem.at[c], device)
                else:
                    pltpu.make_async_copy(own_sum.at[rows], place, up_sem.at[c]).start()

        def back_x(c):
            mine = sum_done.at[place_of(c, x, 0, True)]
            wait_for(mine, up_sem.at[c])
            for j in range(1, side):
                device = {"dp": lax.rem(x + j, side) * other_side + y}
                send(mine, mine, send_sem.at[5, 1], out_sem.at[0], device)

        for c in range(len(chunks)):
            along_x(c)
        stages = (along_y, back_y, back_x)
        for step in range(len(chunks) + len(stages) - 1):
            for n in reversed(range(len(stages))):
                if 0 <= step - n < len(chunks):
                    stages[n](step - n)
        others = across_recv.at[pl.ds(0, side - 1)]
        wait_for(others, out_sem.at[0])
        wait_for(others, send_sem.at[4, 0])
        wait_for(others, send_sem.at[5, 1])
        for n in ((4, 1), (5, 0)):
            wait_for(sum_recv.at[pl.ds(0, other_side - 1)], send_sem.at[n])

    result = pltpu.make_async_copy(sum_done.at[pl.ds(0, out_ref.shape[0])], out_ref, out_sem.at[1])
    result.start()

    for latent in range(latents_here):

        @pl.when(section < last)
        def _(latent=latent):
            wait_for(part_send.at[latent], send_sem.at[0, latent])
            wait_for(shift_send.at[latent], send_sem.at[2, latent])

        @pl.when(section == last)
        def _(latent=latent):
            others = part_send.at[latent, pl.ds(0, shards - 1)]
            wait_for(others, send_sem.at[0, latent])
            wait_for(others, send_sem.at[3, latent])

        @pl.when(section > 0)
        def _(latent=latent):
            wait_for(part_send.at[latent], send_sem.at[1, latent])

    result.wait()


def body(latents, target, base_weight, seeds, timesteps, time_table):
    replicas, sections, shards = (lax.axis_size(name) for name in ("dp", "section", "tensor"))
    channels, latents_here, pixels = latents.shape
    wide = base_weight.shape[3]
    rows = 9 * channels
    piece = sum(PIECES)
    side = min(SIDE, replicas)
    strip = piece * (replicas // side)
    sizes = (replicas, sections, shards, latents_here, latents_here * replicas)
    hbm = pl.BlockSpec(memory_space=pltpu.HBM)
    bf16, f32 = jnp.bfloat16, jnp.float32
    here = latents_here
    scratch = [
        pltpu.VMEM((here, channels, pixels), bf16),
        pltpu.VMEM((here, channels, pixels), bf16),
        pltpu.VMEM((9, channels, wide), bf16),
        pltpu.VMEM(time_table.shape[:0:-1], bf16),
        pltpu.SMEM((1,), jnp.int32),
        pltpu.SMEM((here,), jnp.int32),
        pltpu.SemaphoreType.DMA((6,)),
        pltpu.VMEM((rows, wide), bf16),
        pltpu.VMEM((wide, rows), bf16),
        pltpu.VMEM((here, channels, 128), f32),
        pltpu.VMEM((here, shards, channels, pixels), bf16),
        pltpu.VMEM((2, here, shards, channels, pixels), bf16),
        pltpu.VMEM((here, channels, pixels), f32),
        pltpu.VMEM((here, channels, pixels), f32),
        pltpu.VMEM((2, here, channels, pixels), bf16),
        pltpu.VMEM((here, shards, channels, pixels), bf16),
        pltpu.VMEM((here, rows, pixels), bf16),
        pltpu.VMEM((here, channels, pixels), f32),
        pltpu.VMEM((here, channels, 128), f32),
        pltpu.VMEM((here, channels, pixels), f32),
        pltpu.VMEM((channels, pixels), f32),
        pltpu.VMEM((rows, wide), f32),
        pltpu.VMEM((replicas * piece, wide), bf16),
        pltpu.VMEM((replicas, piece, wide), bf16),
        pltpu.VMEM((piece, wide), bf16),
        pltpu.VMEM((side, strip, wide), bf16),
        pltpu.VMEM((strip, wide), bf16),
        pltpu.VMEM((replicas * piece, wide), bf16),
        pltpu.SemaphoreType.DMA((len(PIECES),)),
        pltpu.SemaphoreType.DMA((len(PIECES),)),
        pltpu.SemaphoreType.DMA((2, here)),
        pltpu.SemaphoreType.DMA((here,)),
        pltpu.SemaphoreType.DMA((here,)),
        pltpu.SemaphoreType.DMA((len(PIECES),)),
        pltpu.SemaphoreType.DMA((2,)),
        pltpu.SemaphoreType.DMA((6, 2)),
    ]
    result = pl.pallas_call(
        functools.partial(kernel, sizes),
        out_shape=jax.ShapeDtypeStruct((rows, wide), bf16),
        in_specs=[hbm] * 6,
        out_specs=hbm,
        scratch_shapes=scratch,
        compiler_params=pltpu.CompilerParams(
            collective_id=0, has_side_effects=True, vmem_limit_bytes=63 * 1024 * 1024
        ),
        cost_estimate=pl.CostEstimate(
            flops=6 * here * rows * wide * pixels, bytes_accessed=4 * rows * wide, transcendentals=0
        ),
    )(
        latents.transpose(1, 0, 2),
        target.transpose(1, 0, 2),
        base_weight[0].transpose(1, 0, 2),
        seeds,
        timesteps,
        time_table[0].T,
    )
    return result.astype(f32).reshape(9, channels, wide).transpose(1, 0, 2)[None]


def solution(mesh):
    in_specs = (
        P("tensor", "dp", None),
        P("tensor", "dp", None),
        P("section", "tensor", None, None),
        P("section"),
        P("dp"),
        P("section", None, "tensor"),
    )
    out_specs = P("section", "tensor", None, None)
    return jax.shard_map(body, mesh=mesh, in_specs=in_specs, out_specs=out_specs, check_vma=False)
```

```python
import functools

import jax
import jax.numpy as jnp
from jax import lax
from jax.experimental import pallas as pl
from jax.experimental.pallas import tpu as pltpu
from jax.sharding import PartitionSpec as P

GROUP = 20
RES = 16
MOD = 65521
PIECES = (32, 16)
SIDE = 4
MESH = pl.DeviceIdType.MESH


def below_mod(value):
    value = (value >> 16) * 15 + (value & 65535)
    value = (value >> 16) * 15 + (value & 65535)
    return jnp.where(value >= MOD, value - MOD, value)


def group_sums(values_list, group):
    rows, lanes = values_list[0].shape
    groups = rows // group
    parts = []
    for values in values_list:
        while values.shape[1] > 128:
            half = values.shape[1] // 2
            values = values[:, :half] + values[:, half:]
        for g in range(groups):
            first, last = g * group, (g + 1) * group
            start, end = first // 8 * 8, -(-last // 8) * 8
            total = None
            for row in range(start, end, 8):
                tile = values[row : row + 8]
                if row < first or row + 8 > last:
                    place = lax.broadcasted_iota(jnp.int32, tile.shape, 0) + row
                    tile = jnp.where((place >= first) & (place < last), tile, 0.0)
                total = tile if total is None else total + tile
            parts.append(jnp.sum(total, axis=0, keepdims=True))
    sums = jnp.sum(jnp.concatenate(parts, axis=0), axis=1, keepdims=True)
    place = lax.broadcasted_iota(jnp.int32, (rows, 1), 0)
    spread = []
    for index in range(len(values_list)):
        base = index * groups
        result = jnp.broadcast_to(sums[base : base + 1], (rows, 1))
        for g in range(1, groups):
            result = jnp.where(place >= g * group, sums[base + g : base + g + 1], result)
        spread.append(result)
    return spread


def tap_masks(pixels):
    place = lax.broadcasted_iota(jnp.int32, (1, pixels), 1)
    row, col = place // RES, place % RES
    return {-1: (row >= 1, col >= 1), 0: (None, None), 1: (row < RES - 1, col < RES - 1)}


def moved(values, offset):
    pixels = values.shape[1]
    return values if offset % pixels == 0 else pltpu.roll(values, (-offset) % pixels, axis=1)


def kernel(
    sizes,
    latents_hbm,
    target_hbm,
    base_hbm,
    seed_hbm,
    steps_hbm,
    table_hbm,
    out_ref,
    latents_ref,
    target_ref,
    base_ref,
    table_ref,
    seed_ref,
    steps_ref,
    load_sem,
    weight,
    weight_t,
    bias,
    part_send,
    part_recv,
    shift_send,
    shift_recv,
    grad_send,
    grad_recv,
    columns,
    normed,
    scale,
    slope,
    held,
    total,
    sum_send,
    sum_recv,
    own_sum,
    across_recv,
    across_sum,
    sum_done,
    down_sem,
    up_sem,
    part_sem,
    shift_sem,
    grad_sem,
    sum_sem,
    out_sem,
    send_sem,
):
    replicas, sections, shards, latents_here, all_latents = sizes
    dp = lax.axis_index("dp")
    section = lax.axis_index("section")
    shard = lax.axis_index("tensor")
    channels, pixels = held.shape
    wide = weight.shape[1]
    last = sections - 1
    side = across_recv.shape[0]
    other_side = replicas // side
    x, y = dp // other_side, lax.rem(dp, other_side)
    chunks, start = [], 0
    for piece in PIECES:
        chunks.append((start, piece))
        start += piece * replicas

    loads = [
        pltpu.make_async_copy(source, place, load_sem.at[n])
        for n, (source, place) in enumerate(
            [
                (steps_hbm, steps_ref),
                (seed_hbm, seed_ref),
                (table_hbm, table_ref),
                (latents_hbm, latents_ref),
                (base_hbm, base_ref),
                (target_hbm, target_ref),
            ]
        )
    ]
    for load in loads:
        load.start()

    barrier = pltpu.get_barrier_semaphore()

    def greet(section_to, skip_own):
        for j in range(1 if skip_own else 0, shards):
            peer = lax.rem(shard + j, shards)
            pl.semaphore_signal(
                barrier,
                inc=1,
                device_id={"section": section_to, "tensor": peer},
                device_id_type=MESH,
            )

    @pl.when(section > 0)
    def _():
        greet(section - 1, False)

    @pl.when(section < last)
    def _():
        greet(section + 1, False)

    @pl.when(section == last)
    def _():
        greet(section, True)

    for j in range(1, replicas):
        pl.semaphore_signal(
            barrier, inc=1, device_id={"dp": lax.rem(dp + j, replicas)}, device_id_type=MESH
        )

    masks = tap_masks(pixels)
    count = float(GROUP * pixels)

    def wait_for(ref, sem):
        pltpu.make_async_copy(ref, ref, sem).wait()

    def send(source, place, sent, arrived, device):
        pltpu.make_async_remote_copy(
            src_ref=source,
            dst_ref=place,
            send_sem=sent,
            recv_sem=arrived,
            device_id=device,
            device_id_type=MESH,
        ).start()

    order = [j for j in (4, 3, 5, 2, 6, 1, 7, 0) if j < shards]
    order += [j for j in range(shards) if j not in order]

    def make_part(latent, peer):
        rows = pl.ds(pl.multiple_of(peer * channels, 16), channels)
        part_send[latent, peer] = jnp.dot(
            weight_t[rows], columns[latent], preferred_element_type=jnp.float32
        ).astype(jnp.bfloat16)

    def send_parts(latent):
        @pl.when(section < last)
        def _():
            for j in order:
                peer = lax.rem(shard + j, shards)
                make_part(latent, peer)
                send(
                    part_send.at[latent, peer],
                    part_recv.at[0, latent, shard],
                    send_sem.at[0, latent],
                    part_sem.at[0, latent],
                    {"section": section + 1, "tensor": peer},
                )

        @pl.when(section == last)
        def _():
            for j in order:
                peer = lax.rem(shard + j, shards)
                make_part(latent, peer)
                if j:
                    send(
                        part_send.at[latent, peer],
                        part_recv.at[1, latent, shard],
                        send_sem.at[0, latent],
                        part_sem.at[1, latent],
                        {"tensor": peer},
                    )
                else:
                    pltpu.make_async_copy(
                        part_send.at[latent, shard],
                        part_recv.at[1, latent, shard],
                        part_sem.at[1, latent],
                    ).start()

    def summed(phase, latent, start):
        result = start
        for j in range(shards):
            result = result + part_recv[phase, latent, j].astype(jnp.float32)
        return result.astype(jnp.bfloat16)

    def take(latent):
        @pl.when(section == 0)
        def _():
            held[...] = latents_ref[latent].astype(jnp.float32)

        @pl.when(section > 0)
        def _():
            wait_for(shift_recv.at[latent], shift_sem.at[latent])
            wait_for(part_recv.at[0, latent], part_sem.at[0, latent])
            held[...] = summed(0, latent, shift_recv[latent]).astype(jnp.float32)

        shift_send[latent] = held[...] + bias[latent][:, 0:1]

    def send_shift(latent):
        @pl.when(section < last)
        def _():
            send(
                shift_send.at[latent],
                shift_recv.at[latent],
                send_sem.at[2, latent],
                shift_sem.at[latent],
                {"section": section + 1},
            )

    def activate(latent):
        shifted = shift_send[latent]
        (sums,) = group_sums([shifted], GROUP)
        center = shifted - sums / count
        (squares,) = group_sums([center * center], GROUP)
        factor = lax.rsqrt(squares / count + 1e-05)
        value = center * factor
        sigmoid = 1.0 / (1.0 + jnp.exp(-value))
        activation = (value * sigmoid).astype(jnp.bfloat16).astype(jnp.float32)
        for dj in (-1, 0, 1):
            across = moved(activation, dj)
            if dj:
                across = jnp.where(masks[dj][1], across, 0.0)
            for di in (-1, 0, 1):
                tap = (di + 1) * 3 + dj + 1
                both = moved(across, di * RES)
                if di:
                    both = jnp.where(masks[di][0], both, 0.0)
                columns[latent, tap * channels : (tap + 1) * channels] = both.astype(jnp.bfloat16)
        normed[latent] = value
        slope[latent] = sigmoid
        scale[latent] = jnp.broadcast_to(factor, (channels, 128))

    def emit(latent):
        send_parts(latent)
        sigmoid = slope[latent]
        slope[latent] = sigmoid * (1.0 + normed[latent] * (1.0 - sigmoid))

    loads[0].wait()
    loads[2].wait()
    loads[3].wait()
    table_step = lax.broadcasted_iota(jnp.int32, table_ref.shape, 1)
    table = table_ref[...].astype(jnp.float32)
    for latent in range(latents_here):
        picked = jnp.where(table_step == steps_ref[latent], table, 0.0)
        own_bias = jnp.broadcast_to(jnp.sum(picked, axis=1, keepdims=True), (channels, 128))
        bias[latent] = own_bias

    @pl.when(section == 0)
    def _():
        take(0)
        activate(0)

    for n in (1, 4, 5):
        loads[n].wait()
    seed = seed_ref[0]
    out_channel = lax.broadcasted_iota(jnp.int32, (8, wide), 1)
    out_part = below_mod(out_channel[0:1] * 32749)
    row_channel = lax.broadcasted_iota(jnp.int32, (channels, 128), 0) + shard * channels
    lane = lax.broadcasted_iota(jnp.int32, (channels, 128), 1)
    for tap in range(9):
        first_index = (row_channel * 9 + tap) * wide
        high = first_index >> 16
        low = high * 15 + (first_index & 65535)
        over = low >= MOD
        low = jnp.where(over, low - MOD, low)
        high = jnp.where(over, high + 1, high)
        row_part = below_mod(low * 32749 + high * 12345 + seed)
        for col in range(0, wide, 128):
            size = min(128, wide - col)
            mixed = row_part[:, :size] + out_part[:, col : col + size]
            mixed = jnp.where(low[:, :size] + lane[:, :size] >= MOD - col, mixed + 12345, mixed)
            mixed = jnp.where(mixed >= MOD, mixed - MOD, mixed)
            mixed = jnp.where(mixed >= MOD, mixed - MOD, mixed)
            noise = mixed.astype(jnp.float32) / 65521.0 - 0.5
            weight[tap * channels : (tap + 1) * channels, col : col + size] = (
                base_ref[tap, :, col : col + size].astype(jnp.float32) + 0.02 * noise
            ).astype(jnp.bfloat16)
    weight_t[...] = weight[...].T

    for s in range(sections):
        amount = replicas - 1 + shards * ((s > 0) + (s < last)) + (shards - 1) * (s == last)

        @pl.when(section == s)
        def _(amount=amount):
            pl.semaphore_wait(barrier, amount)

    @pl.when(section > 0)
    def _():
        take(0)
        send_shift(0)
        activate(0)

    @pl.when(section == 0)
    def _():
        send_shift(0)

    emit(0)
    for latent in range(1, latents_here):
        take(latent)
        send_shift(latent)
        activate(latent)
        emit(latent)

    grad_back = grad_send.at[1]
    grad_first = grad_send.at[0]

    for latent in range(latents_here):

        @pl.when(section == last)
        def _(latent=latent):
            wait_for(part_recv.at[1, latent], part_sem.at[1, latent])
            output = summed(1, latent, shift_send[latent]).astype(jnp.float32)
            grad_first[latent] = (
                (output - target_ref[latent].astype(jnp.float32)) / float(all_latents)
            ).astype(jnp.bfloat16)
            for j in order:
                peer = lax.rem(shard + j, shards)
                if j:
                    send(
                        grad_first.at[latent],
                        grad_recv.at[latent, shard],
                        send_sem.at[3, latent],
                        grad_sem.at[latent],
                        {"tensor": peer},
                    )
                else:
                    pltpu.make_async_copy(
                        grad_first.at[latent], grad_recv.at[latent, shard], grad_sem.at[latent]
                    ).start()

    for latent in range(latents_here):
        wait_for(grad_recv.at[latent], grad_sem.at[latent])
        out_grad = grad_recv[latent].reshape(wide, pixels)

        @pl.when(section > 0)
        def _(latent=latent, out_grad=out_grad):
            spread = jnp.dot(weight[...], out_grad, preferred_element_type=jnp.float32)
            col_grad = None
            for dj in (-1, 0, 1):
                down = None
                for di in (-1, 0, 1):
                    tap = (di + 1) * 3 + dj + 1
                    term = spread[tap * channels : (tap + 1) * channels]
                    if di:
                        term = moved(jnp.where(masks[di][0], term, 0.0), -di * RES)
                    down = term if down is None else down + term
                if dj:
                    down = moved(jnp.where(masks[dj][1], down, 0.0), -dj)
                col_grad = down if col_grad is None else col_grad + down
            value = normed[latent]
            inner = col_grad * slope[latent]
            mean_inner, mean_both = group_sums([inner, inner * value], GROUP)
            in_grad = scale[latent][:, 0:1] * (
                inner - mean_inner / count - value * (mean_both / count)
            )
            grad_back[latent] = (
                grad_recv[latent, shard].astype(jnp.float32) + in_grad
            ).astype(jnp.bfloat16)
            for j in order:
                send(
                    grad_back.at[latent],
                    grad_recv.at[latent, shard],
                    send_sem.at[1, latent],
                    grad_sem.at[latent],
                    {
                        "section": section - 1,
                        "tensor": lax.rem(shard + j, shards),
                    },
                )

        part = lax.dot_general(
            columns[latent], out_grad, (((1,), (1,)), ((), ())), preferred_element_type=jnp.float32
        )
        if latent == 0 and latents_here > 1:
            total[...] = part
        elif latent < latents_here - 1:
            total[...] += part
        else:
            if latent:
                part = total[...] + part
            rows = part.shape[0]
            sum_send[:rows] = part.astype(jnp.bfloat16)
            if rows < sum_send.shape[0]:
                sum_send[rows:] = jnp.zeros((sum_send.shape[0] - rows, wide), jnp.bfloat16)

    def added(ref, rows):
        result = ref[0, rows].astype(jnp.float32)
        for j in range(1, ref.shape[0]):
            result = result + ref[j, rows].astype(jnp.float32)
        return result.astype(jnp.bfloat16)

    def place_of(c, x_to, y_to, strip=False):
        start, piece = chunks[c]
        row = start + (x_to * other_side + y_to) * piece
        return pl.ds(pl.multiple_of(row, 16), piece * (other_side if strip else 1))

    def kept(c, strip=False):
        start, piece = chunks[c]
        scale_by = side if strip else replicas
        return pl.ds(start // scale_by, piece * (other_side if strip else 1))

    def around(size):
        return sorted(range(size), key=lambda j: -min(j, size - j))

    steps = [(i, j) for i in range(side) for j in range(other_side)]
    steps.sort(key=lambda ij: -min(ij[0], side - ij[0]) - 2 * min(ij[1], other_side - ij[1]))
    far_first = [
        (i + j, lax.rem(x + i, side) * other_side + lax.rem(y + j, other_side)) for i, j in steps
    ]

    @pl.when(section == 0)
    def _():
        for c in range(len(chunks)):
            for j, owner in far_first:
                source = sum_send.at[place_of(c, 0, owner)]
                place = sum_recv.at[dp, kept(c)]
                if j:
                    send(source, place, send_sem.at[4, 0], sum_sem.at[c], {"dp": owner})
                else:
                    pltpu.make_async_copy(source, place, sum_sem.at[c]).start()
        for c in range(len(chunks)):
            rows = kept(c)
            wait_for(sum_recv.at[:, rows], sum_sem.at[c])
            own_sum[rows] = added(sum_recv, rows)
            place = sum_done.at[place_of(c, 0, dp)]
            for j, other in far_first:
                if j:
                    send(
                        own_sum.at[rows], place, send_sem.at[4, 1], out_sem.at[0], {"dp": other}
                    )
                else:
                    pltpu.make_async_copy(own_sum.at[rows], place, out_sem.at[0]).start()
        wait_for(sum_done, out_sem.at[0])
        wait_for(sum_recv.at[pl.ds(0, replicas - 1)], send_sem.at[4, 0])
        wait_for(sum_recv.at[pl.ds(0, replicas - 1)], send_sem.at[4, 1])

    @pl.when(section > 0)
    def _():
        def along_x(c):
            for j in around(side):
                to = lax.rem(x + j, side)
                source = sum_send.at[place_of(c, to, 0, True)]
                place = across_recv.at[x, kept(c, True)]
                if j:
                    device = {"dp": to * other_side + y}
                    send(source, place, send_sem.at[4, 0], sum_sem.at[c], device)
                else:
                    pltpu.make_async_copy(source, place, sum_sem.at[c]).start()

        def along_y(c):
            start, piece = chunks[c]
            rows = kept(c, True)
            wait_for(across_recv.at[:, rows], sum_sem.at[c])
            across_sum[rows] = added(across_recv, rows)
            for j in around(other_side):
                to = lax.rem(y + j, other_side)
                row = pl.multiple_of(start // side + to * piece, 16)
                source = across_sum.at[pl.ds(row, piece)]
                place = sum_recv.at[y, kept(c)]
                if j:
                    device = {"dp": x * other_side + to}
                    send(source, place, send_sem.at[4, 1], down_sem.at[c], device)
                else:
                    pltpu.make_async_copy(source, place, down_sem.at[c]).start()

        def back_y(c):
            rows = kept(c)
            wait_for(sum_recv.at[pl.ds(0, other_side), rows], down_sem.at[c])
            own_sum[rows] = added(sum_recv.at[pl.ds(0, other_side)], rows)
            place = sum_done.at[place_of(c, x, y)]
            for j in around(other_side):
                if j:
                    device = {"dp": x * other_side + lax.rem(y + j, other_side)}
                    send(own_sum.at[rows], place, send_sem.at[5, 0], up_sem.at[c], device)
                else:
                    pltpu.make_async_copy(own_sum.at[rows], place, up_sem.at[c]).start()

        def back_x(c):
            mine = sum_done.at[place_of(c, x, 0, True)]
            wait_for(mine, up_sem.at[c])
            for j in around(side)[:-1]:
                device = {"dp": lax.rem(x + j, side) * other_side + y}
                send(mine, mine, send_sem.at[5, 1], out_sem.at[0], device)

        for c in range(len(chunks)):
            along_x(c)
        stages = (along_y, back_y, back_x)
        for step in range(len(chunks) + len(stages) - 1):
            for n in reversed(range(len(stages))):
                if 0 <= step - n < len(chunks):
                    stages[n](step - n)
        others = across_recv.at[pl.ds(0, side - 1)]
        wait_for(others, out_sem.at[0])
        wait_for(others, send_sem.at[4, 0])
        wait_for(others, send_sem.at[5, 1])
        for n in ((4, 1), (5, 0)):
            wait_for(sum_recv.at[pl.ds(0, other_side - 1)], send_sem.at[n])

    result = pltpu.make_async_copy(sum_done.at[pl.ds(0, out_ref.shape[0])], out_ref, out_sem.at[1])
    result.start()

    for latent in range(latents_here):

        @pl.when(section < last)
        def _(latent=latent):
            wait_for(part_send.at[latent], send_sem.at[0, latent])
            wait_for(shift_send.at[latent], send_sem.at[2, latent])

        @pl.when(section == last)
        def _(latent=latent):
            others = part_send.at[latent, pl.ds(0, shards - 1)]
            wait_for(others, send_sem.at[0, latent])
            wait_for(others, send_sem.at[3, latent])

        @pl.when(section > 0)
        def _(latent=latent):
            wait_for(part_send.at[latent], send_sem.at[1, latent])

    result.wait()


def body(latents, target, base_weight, seeds, timesteps, time_table):
    replicas, sections, shards = (lax.axis_size(name) for name in ("dp", "section", "tensor"))
    channels, latents_here, pixels = latents.shape
    wide = base_weight.shape[3]
    rows = 9 * channels
    piece = sum(PIECES)
    side = min(SIDE, replicas)
    strip = piece * (replicas // side)
    sizes = (replicas, sections, shards, latents_here, latents_here * replicas)
    hbm = pl.BlockSpec(memory_space=pltpu.HBM)
    bf16, f32 = jnp.bfloat16, jnp.float32
    here = latents_here
    scratch = [
        pltpu.VMEM((here, channels, pixels), bf16),
        pltpu.VMEM((here, channels, pixels), bf16),
        pltpu.VMEM((9, channels, wide), bf16),
        pltpu.VMEM(time_table.shape[:0:-1], bf16),
        pltpu.SMEM((1,), jnp.int32),
        pltpu.SMEM((here,), jnp.int32),
        pltpu.SemaphoreType.DMA((6,)),
        pltpu.VMEM((rows, wide), bf16),
        pltpu.VMEM((wide, rows), bf16),
        pltpu.VMEM((here, channels, 128), f32),
        pltpu.VMEM((here, shards, channels, pixels), bf16),
        pltpu.VMEM((2, here, shards, channels, pixels), bf16),
        pltpu.VMEM((here, channels, pixels), f32),
        pltpu.VMEM((here, channels, pixels), f32),
        pltpu.VMEM((2, here, channels, pixels), bf16),
        pltpu.VMEM((here, shards, channels, pixels), bf16),
        pltpu.VMEM((here, rows, pixels), bf16),
        pltpu.VMEM((here, channels, pixels), f32),
        pltpu.VMEM((here, channels, 128), f32),
        pltpu.VMEM((here, channels, pixels), f32),
        pltpu.VMEM((channels, pixels), f32),
        pltpu.VMEM((rows, wide), f32),
        pltpu.VMEM((replicas * piece, wide), bf16),
        pltpu.VMEM((replicas, piece, wide), bf16),
        pltpu.VMEM((piece, wide), bf16),
        pltpu.VMEM((side, strip, wide), bf16),
        pltpu.VMEM((strip, wide), bf16),
        pltpu.VMEM((replicas * piece, wide), bf16),
        pltpu.SemaphoreType.DMA((len(PIECES),)),
        pltpu.SemaphoreType.DMA((len(PIECES),)),
        pltpu.SemaphoreType.DMA((2, here)),
        pltpu.SemaphoreType.DMA((here,)),
        pltpu.SemaphoreType.DMA((here,)),
        pltpu.SemaphoreType.DMA((len(PIECES),)),
        pltpu.SemaphoreType.DMA((2,)),
        pltpu.SemaphoreType.DMA((6, 2)),
    ]
    result = pl.pallas_call(
        functools.partial(kernel, sizes),
        out_shape=jax.ShapeDtypeStruct((rows, wide), bf16),
        in_specs=[hbm] * 6,
        out_specs=hbm,
        scratch_shapes=scratch,
        compiler_params=pltpu.CompilerParams(
            collective_id=0, has_side_effects=True, vmem_limit_bytes=63 * 1024 * 1024
        ),
        cost_estimate=pl.CostEstimate(
            flops=6 * here * rows * wide * pixels, bytes_accessed=4 * rows * wide, transcendentals=0
        ),
    )(
        latents.transpose(1, 0, 2),
        target.transpose(1, 0, 2),
        base_weight[0].transpose(1, 0, 2),
        seeds,
        timesteps,
        time_table[0].T,
    )
    return result.astype(f32).reshape(9, channels, wide).transpose(1, 0, 2)[None]


def solution(mesh):
    in_specs = (
        P("tensor", "dp", None),
        P("tensor", "dp", None),
        P("section", "tensor", None, None),
        P("section"),
        P("dp"),
        P("section", None, "tensor"),
    )
    out_specs = P("section", "tensor", None, None)
    return jax.shard_map(body, mesh=mesh, in_specs=in_specs, out_specs=out_specs, check_vma=False)
```

```python
import functools

import jax
import jax.numpy as jnp
from jax import lax
from jax.experimental import pallas as pl
from jax.experimental.pallas import tpu as pltpu
from jax.sharding import PartitionSpec as P

GROUP = 20
RES = 16
MOD = 65521
PIECES = (32, 16)
SIDE = 4
MESH = pl.DeviceIdType.MESH


def below_mod(value):
    value = (value >> 16) * 15 + (value & 65535)
    value = (value >> 16) * 15 + (value & 65535)
    return jnp.where(value >= MOD, value - MOD, value)


def group_sums(values_list, group):
    rows, lanes = values_list[0].shape
    groups = rows // group
    parts = []
    for values in values_list:
        while values.shape[1] > 128:
            half = values.shape[1] // 2
            values = values[:, :half] + values[:, half:]
        for g in range(groups):
            first, last = g * group, (g + 1) * group
            start, end = first // 8 * 8, -(-last // 8) * 8
            total = None
            for row in range(start, end, 8):
                tile = values[row : row + 8]
                if row < first or row + 8 > last:
                    place = lax.broadcasted_iota(jnp.int32, tile.shape, 0) + row
                    tile = jnp.where((place >= first) & (place < last), tile, 0.0)
                total = tile if total is None else total + tile
            parts.append(jnp.sum(total, axis=0, keepdims=True))
    sums = jnp.sum(jnp.concatenate(parts, axis=0), axis=1, keepdims=True)
    place = lax.broadcasted_iota(jnp.int32, (rows, 1), 0)
    spread = []
    for index in range(len(values_list)):
        base = index * groups
        result = jnp.broadcast_to(sums[base : base + 1], (rows, 1))
        for g in range(1, groups):
            result = jnp.where(place >= g * group, sums[base + g : base + g + 1], result)
        spread.append(result)
    return spread


def tap_masks(pixels):
    place = lax.broadcasted_iota(jnp.int32, (1, pixels), 1)
    row, col = place // RES, place % RES
    return {-1: (row >= 1, col >= 1), 0: (None, None), 1: (row < RES - 1, col < RES - 1)}


def moved(values, offset):
    pixels = values.shape[1]
    return values if offset % pixels == 0 else pltpu.roll(values, (-offset) % pixels, axis=1)


def kernel(
    sizes,
    latents_hbm,
    target_hbm,
    base_hbm,
    seed_hbm,
    steps_hbm,
    table_hbm,
    out_ref,
    latents_ref,
    target_ref,
    base_ref,
    table_ref,
    seed_ref,
    steps_ref,
    load_sem,
    weight,
    weight_t,
    bias,
    part_send,
    part_recv,
    shift_send,
    shift_recv,
    grad_send,
    grad_recv,
    columns,
    normed,
    scale,
    slope,
    held,
    total,
    sum_send,
    sum_recv,
    own_sum,
    across_recv,
    across_sum,
    sum_done,
    down_sem,
    up_sem,
    part_sem,
    shift_sem,
    grad_sem,
    sum_sem,
    out_sem,
    send_sem,
):
    replicas, sections, shards, latents_here, all_latents = sizes
    dp = lax.axis_index("dp")
    section = lax.axis_index("section")
    shard = lax.axis_index("tensor")
    channels, pixels = held.shape
    wide = weight.shape[1]
    last = sections - 1
    side = across_recv.shape[0]
    other_side = replicas // side
    x, y = dp // other_side, lax.rem(dp, other_side)
    chunks, start = [], 0
    for piece in PIECES:
        chunks.append((start, piece))
        start += piece * replicas

    loads = [
        pltpu.make_async_copy(source, place, load_sem.at[n])
        for n, (source, place) in enumerate(
            [
                (steps_hbm, steps_ref),
                (seed_hbm, seed_ref),
                (table_hbm, table_ref),
                (latents_hbm, latents_ref),
                (base_hbm, base_ref),
                (target_hbm, target_ref),
            ]
        )
    ]
    for load in loads:
        load.start()

    barrier = pltpu.get_barrier_semaphore()

    def greet(section_to, skip_own):
        for j in range(1 if skip_own else 0, shards):
            peer = lax.rem(shard + j, shards)
            pl.semaphore_signal(
                barrier,
                inc=1,
                device_id={"section": section_to, "tensor": peer},
                device_id_type=MESH,
            )

    @pl.when(section > 0)
    def _():
        greet(section - 1, False)

    @pl.when(section < last)
    def _():
        greet(section + 1, False)

    @pl.when(section == last)
    def _():
        greet(section, True)

    for j in range(1, replicas):
        pl.semaphore_signal(
            barrier, inc=1, device_id={"dp": lax.rem(dp + j, replicas)}, device_id_type=MESH
        )

    masks = tap_masks(pixels)
    count = float(GROUP * pixels)

    def wait_for(ref, sem):
        pltpu.make_async_copy(ref, ref, sem).wait()

    def send(source, place, sent, arrived, device):
        pltpu.make_async_remote_copy(
            src_ref=source,
            dst_ref=place,
            send_sem=sent,
            recv_sem=arrived,
            device_id=device,
            device_id_type=MESH,
        ).start()

    order = [j for j in (4, 3, 5, 2, 6, 1, 7, 0) if j < shards]
    order += [j for j in range(shards) if j not in order]

    def make_part(latent, peer):
        rows = pl.ds(pl.multiple_of(peer * channels, 16), channels)
        part_send[latent, peer] = jnp.dot(
            weight_t[rows], columns[latent], preferred_element_type=jnp.float32
        ).astype(jnp.bfloat16)

    def send_parts(latent):
        @pl.when(section < last)
        def _():
            for j in order:
                peer = lax.rem(shard + j, shards)
                make_part(latent, peer)
                send(
                    part_send.at[latent, peer],
                    part_recv.at[0, latent, shard],
                    send_sem.at[0, latent],
                    part_sem.at[0, latent],
                    {"section": section + 1, "tensor": peer},
                )

        @pl.when(section == last)
        def _():
            for j in order:
                peer = lax.rem(shard + j, shards)
                make_part(latent, peer)
                if j:
                    send(
                        part_send.at[latent, peer],
                        part_recv.at[1, latent, shard],
                        send_sem.at[0, latent],
                        part_sem.at[1, latent],
                        {"tensor": peer},
                    )
                else:
                    pltpu.make_async_copy(
                        part_send.at[latent, shard],
                        part_recv.at[1, latent, shard],
                        part_sem.at[1, latent],
                    ).start()

    def summed(phase, latent, start):
        result = start
        for j in range(shards):
            result = result + part_recv[phase, latent, j].astype(jnp.float32)
        return result.astype(jnp.bfloat16)

    def take(latent):
        @pl.when(section == 0)
        def _():
            held[...] = latents_ref[...].astype(jnp.float32)[:, latent]

        @pl.when(section > 0)
        def _():
            wait_for(shift_recv.at[latent], shift_sem.at[latent])
            wait_for(part_recv.at[0, latent], part_sem.at[0, latent])
            held[...] = summed(0, latent, shift_recv[latent]).astype(jnp.float32)

        shift_send[latent] = held[...] + bias[latent][:, 0:1]

    def send_shift(latent):
        @pl.when(section < last)
        def _():
            send(
                shift_send.at[latent],
                shift_recv.at[latent],
                send_sem.at[2, latent],
                shift_sem.at[latent],
                {"section": section + 1},
            )

    def activate(latent):
        shifted = shift_send[latent]
        (sums,) = group_sums([shifted], GROUP)
        center = shifted - sums / count
        (squares,) = group_sums([center * center], GROUP)
        factor = lax.rsqrt(squares / count + 1e-05)
        value = center * factor
        sigmoid = 1.0 / (1.0 + jnp.exp(-value))
        activation = (value * sigmoid).astype(jnp.bfloat16).astype(jnp.float32)
        for dj in (-1, 0, 1):
            across = moved(activation, dj)
            if dj:
                across = jnp.where(masks[dj][1], across, 0.0)
            for di in (-1, 0, 1):
                tap = (di + 1) * 3 + dj + 1
                both = moved(across, di * RES)
                if di:
                    both = jnp.where(masks[di][0], both, 0.0)
                columns[latent, tap * channels : (tap + 1) * channels] = both.astype(jnp.bfloat16)
        normed[latent] = value
        slope[latent] = sigmoid
        scale[latent] = jnp.broadcast_to(factor, (channels, 128))

    def emit(latent):
        send_parts(latent)
        sigmoid = slope[latent]
        slope[latent] = sigmoid * (1.0 + normed[latent] * (1.0 - sigmoid))

    loads[0].wait()
    loads[2].wait()
    loads[3].wait()
    table_step = lax.broadcasted_iota(jnp.int32, table_ref.shape, 1)
    table = table_ref[...].astype(jnp.float32)
    for latent in range(latents_here):
        picked = jnp.where(table_step == steps_ref[latent], table, 0.0)
        own_bias = jnp.broadcast_to(jnp.sum(picked, axis=1, keepdims=True), (channels, 128))
        bias[latent] = own_bias

    @pl.when(section == 0)
    def _():
        take(0)
        activate(0)

    for n in (1, 4, 5):
        loads[n].wait()
    seed = seed_ref[0]
    out_channel = lax.broadcasted_iota(jnp.int32, (8, wide), 1)
    out_part = below_mod(out_channel[0:1] * 32749)
    row_channel = lax.broadcasted_iota(jnp.int32, (channels, 128), 0) + shard * channels
    lane = lax.broadcasted_iota(jnp.int32, (channels, 128), 1)
    for tap in range(9):
        first_index = (row_channel * 9 + tap) * wide
        high = first_index >> 16
        low = high * 15 + (first_index & 65535)
        over = low >= MOD
        low = jnp.where(over, low - MOD, low)
        high = jnp.where(over, high + 1, high)
        row_part = below_mod(low * 32749 + high * 12345 + seed)
        for col in range(0, wide, 128):
            size = min(128, wide - col)
            mixed = row_part[:, :size] + out_part[:, col : col + size]
            mixed = jnp.where(low[:, :size] + lane[:, :size] >= MOD - col, mixed + 12345, mixed)
            mixed = jnp.where(mixed >= MOD, mixed - MOD, mixed)
            mixed = jnp.where(mixed >= MOD, mixed - MOD, mixed)
            noise = mixed.astype(jnp.float32) / 65521.0 - 0.5
            weight[tap * channels : (tap + 1) * channels, col : col + size] = (
                base_ref[tap, :, col : col + size].astype(jnp.float32) + 0.02 * noise
            ).astype(jnp.bfloat16)
    weight_t[...] = weight[...].T

    for s in range(sections):
        amount = replicas - 1 + shards * ((s > 0) + (s < last)) + (shards - 1) * (s == last)

        @pl.when(section == s)
        def _(amount=amount):
            pl.semaphore_wait(barrier, amount)

    @pl.when(section > 0)
    def _():
        take(0)
        send_shift(0)
        activate(0)

    @pl.when(section == 0)
    def _():
        send_shift(0)

    emit(0)
    for latent in range(1, latents_here):
        take(latent)
        send_shift(latent)
        activate(latent)
        emit(latent)

    grad_back = grad_send.at[1]
    grad_first = grad_send.at[0]

    for latent in range(latents_here):

        @pl.when(section == last)
        def _(latent=latent):
            wait_for(part_recv.at[1, latent], part_sem.at[1, latent])
            output = summed(1, latent, shift_send[latent]).astype(jnp.float32)
            grad_first[latent] = (
                (output - target_ref[...].astype(jnp.float32)[:, latent]) / float(all_latents)
            ).astype(jnp.bfloat16)
            for j in order:
                peer = lax.rem(shard + j, shards)
                if j:
                    send(
                        grad_first.at[latent],
                        grad_recv.at[latent, shard],
                        send_sem.at[3, latent],
                        grad_sem.at[latent],
                        {"tensor": peer},
                    )
                else:
                    pltpu.make_async_copy(
                        grad_first.at[latent], grad_recv.at[latent, shard], grad_sem.at[latent]
                    ).start()

    def added(ref, rows):
        result = ref[0, rows].astype(jnp.float32)
        for j in range(1, ref.shape[0]):
            result = result + ref[j, rows].astype(jnp.float32)
        return result.astype(jnp.bfloat16)

    def place_of(c, x_to, y_to, strip=False):
        start, piece = chunks[c]
        row = start + (x_to * other_side + y_to) * piece
        return pl.ds(pl.multiple_of(row, 16), piece * (other_side if strip else 1))

    def kept(c, strip=False):
        start, piece = chunks[c]
        scale_by = side if strip else replicas
        return pl.ds(start // scale_by, piece * (other_side if strip else 1))

    def around(size):
        return sorted(range(size), key=lambda j: -min(j, size - j))

    steps = [(i, j) for i in range(side) for j in range(other_side)]
    steps.sort(key=lambda ij: -min(ij[0], side - ij[0]) - 2 * min(ij[1], other_side - ij[1]))
    far_first = [
        (i + j, lax.rem(x + i, side) * other_side + lax.rem(y + j, other_side)) for i, j in steps
    ]

    def along_x(c):
        for j in around(side):
            to = lax.rem(x + j, side)
            source = sum_send.at[place_of(c, to, 0, True)]
            place = across_recv.at[x, kept(c, True)]
            if j:
                device = {"dp": to * other_side + y}
                send(source, place, send_sem.at[4, 0], sum_sem.at[c], device)
            else:
                pltpu.make_async_copy(source, place, sum_sem.at[c]).start()

    def along_y(c):
        start, piece = chunks[c]
        rows = kept(c, True)
        wait_for(across_recv.at[:, rows], sum_sem.at[c])
        across_sum[rows] = added(across_recv, rows)
        for j in around(other_side):
            to = lax.rem(y + j, other_side)
            row = pl.multiple_of(start // side + to * piece, 16)
            source = across_sum.at[pl.ds(row, piece)]
            place = sum_recv.at[y, kept(c)]
            if j:
                device = {"dp": x * other_side + to}
                send(source, place, send_sem.at[4, 1], down_sem.at[c], device)
            else:
                pltpu.make_async_copy(source, place, down_sem.at[c]).start()

    padding = sum_send.shape[0] - weight.shape[0]
    sum_send[pl.ds(weight.shape[0], padding)] = jnp.zeros((padding, wide), jnp.bfloat16)

    for latent in range(latents_here):
        wait_for(grad_recv.at[latent], grad_sem.at[latent])
        out_grad = grad_recv[latent].reshape(wide, pixels)

        @pl.when(section > 0)
        def _(latent=latent, out_grad=out_grad):
            spread = jnp.dot(weight[...], out_grad, preferred_element_type=jnp.float32)
            col_grad = None
            for dj in (-1, 0, 1):
                down = None
                for di in (-1, 0, 1):
                    tap = (di + 1) * 3 + dj + 1
                    term = spread[tap * channels : (tap + 1) * channels]
                    if di:
                        term = moved(jnp.where(masks[di][0], term, 0.0), -di * RES)
                    down = term if down is None else down + term
                if dj:
                    down = moved(jnp.where(masks[dj][1], down, 0.0), -dj)
                col_grad = down if col_grad is None else col_grad + down
            value = normed[latent]
            inner = col_grad * slope[latent]
            mean_inner, mean_both = group_sums([inner, inner * value], GROUP)
            in_grad = scale[latent][:, 0:1] * (
                inner - mean_inner / count - value * (mean_both / count)
            )
            grad_back[latent] = (
                grad_recv[latent, shard].astype(jnp.float32) + in_grad
            ).astype(jnp.bfloat16)
            for j in order:
                send(
                    grad_back.at[latent],
                    grad_recv.at[latent, shard],
                    send_sem.at[1, latent],
                    grad_sem.at[latent],
                    {
                        "section": section - 1,
                        "tensor": lax.rem(shard + j, shards),
                    },
                )

        for c, (start, piece) in enumerate(chunks):
            rows = pl.ds(start, min(piece * replicas, weight.shape[0] - start))
            part = lax.dot_general(
                columns[latent, rows],
                out_grad,
                (((1,), (1,)), ((), ())),
                preferred_element_type=jnp.float32,
            )
            if latent:
                part = total[rows] + part
            if latent < latents_here - 1:
                total[rows] = part
            else:
                sum_send[rows] = part.astype(jnp.bfloat16)
                along_x(c)

    @pl.when(section == 0)
    def _():
        for c in range(len(chunks)):
            along_y(c)
        for c in range(len(chunks)):
            rows = kept(c)
            wait_for(sum_recv.at[pl.ds(0, other_side), rows], down_sem.at[c])
            own_sum[rows] = added(sum_recv.at[pl.ds(0, other_side)], rows)
            place = sum_done.at[place_of(c, 0, dp)]
            for j, other in far_first:
                if j:
                    send(
                        own_sum.at[rows], place, send_sem.at[5, 0], out_sem.at[0], {"dp": other}
                    )
                else:
                    pltpu.make_async_copy(own_sum.at[rows], place, out_sem.at[0]).start()
        wait_for(sum_done, out_sem.at[0])
        wait_for(across_recv.at[pl.ds(0, side - 1)], send_sem.at[4, 0])
        wait_for(sum_recv.at[pl.ds(0, other_side - 1)], send_sem.at[4, 1])
        wait_for(sum_recv.at[pl.ds(0, replicas - 1)], send_sem.at[5, 0])

    @pl.when(section > 0)
    def _():
        def back_y(c):
            rows = kept(c)
            wait_for(sum_recv.at[pl.ds(0, other_side), rows], down_sem.at[c])
            own_sum[rows] = added(sum_recv.at[pl.ds(0, other_side)], rows)
            place = sum_done.at[place_of(c, x, y)]
            for j in around(other_side):
                if j:
                    device = {"dp": x * other_side + lax.rem(y + j, other_side)}
                    send(own_sum.at[rows], place, send_sem.at[5, 0], up_sem.at[c], device)
                else:
                    pltpu.make_async_copy(own_sum.at[rows], place, up_sem.at[c]).start()

        def back_x(c):
            mine = sum_done.at[place_of(c, x, 0, True)]
            wait_for(mine, up_sem.at[c])
            for j in around(side)[:-1]:
                device = {"dp": lax.rem(x + j, side) * other_side + y}
                send(mine, mine, send_sem.at[5, 1], out_sem.at[0], device)

        stages = (along_y, back_y, back_x)
        for step in range(len(chunks) + len(stages) - 1):
            for n in reversed(range(len(stages))):
                if 0 <= step - n < len(chunks):
                    stages[n](step - n)
        others = across_recv.at[pl.ds(0, side - 1)]
        wait_for(others, out_sem.at[0])
        wait_for(others, send_sem.at[4, 0])
        wait_for(others, send_sem.at[5, 1])
        for n in ((4, 1), (5, 0)):
            wait_for(sum_recv.at[pl.ds(0, other_side - 1)], send_sem.at[n])

    result = pltpu.make_async_copy(sum_done.at[pl.ds(0, out_ref.shape[0])], out_ref, out_sem.at[1])
    result.start()

    for latent in range(latents_here):

        @pl.when(section < last)
        def _(latent=latent):
            wait_for(part_send.at[latent], send_sem.at[0, latent])
            wait_for(shift_send.at[latent], send_sem.at[2, latent])

        @pl.when(section == last)
        def _(latent=latent):
            others = part_send.at[latent, pl.ds(0, shards - 1)]
            wait_for(others, send_sem.at[0, latent])
            wait_for(others, send_sem.at[3, latent])

        @pl.when(section > 0)
        def _(latent=latent):
            wait_for(part_send.at[latent], send_sem.at[1, latent])

    result.wait()


def body(latents, target, base_weight, seeds, timesteps, time_table):
    replicas, sections, shards = (lax.axis_size(name) for name in ("dp", "section", "tensor"))
    channels, latents_here, pixels = latents.shape
    wide = base_weight.shape[3]
    rows = 9 * channels
    piece = sum(PIECES)
    side = min(SIDE, replicas)
    strip = piece * (replicas // side)
    sizes = (replicas, sections, shards, latents_here, latents_here * replicas)
    hbm = pl.BlockSpec(memory_space=pltpu.HBM)
    bf16, f32 = jnp.bfloat16, jnp.float32
    here = latents_here
    scratch = [
        pltpu.VMEM((channels, here, pixels), bf16),
        pltpu.VMEM((channels, here, pixels), bf16),
        pltpu.VMEM((9, channels, wide), bf16),
        pltpu.VMEM(time_table.shape[:0:-1], bf16),
        pltpu.SMEM((1,), jnp.int32),
        pltpu.SMEM((here,), jnp.int32),
        pltpu.SemaphoreType.DMA((6,)),
        pltpu.VMEM((rows, wide), bf16),
        pltpu.VMEM((wide, rows), bf16),
        pltpu.VMEM((here, channels, 128), f32),
        pltpu.VMEM((here, shards, channels, pixels), bf16),
        pltpu.VMEM((2, here, shards, channels, pixels), bf16),
        pltpu.VMEM((here, channels, pixels), f32),
        pltpu.VMEM((here, channels, pixels), f32),
        pltpu.VMEM((2, here, channels, pixels), bf16),
        pltpu.VMEM((here, shards, channels, pixels), bf16),
        pltpu.VMEM((here, rows, pixels), bf16),
        pltpu.VMEM((here, channels, pixels), f32),
        pltpu.VMEM((here, channels, 128), f32),
        pltpu.VMEM((here, channels, pixels), f32),
        pltpu.VMEM((channels, pixels), f32),
        pltpu.VMEM((rows, wide), f32),
        pltpu.VMEM((replicas * piece, wide), bf16),
        pltpu.VMEM((replicas, piece, wide), bf16),
        pltpu.VMEM((piece, wide), bf16),
        pltpu.VMEM((side, strip, wide), bf16),
        pltpu.VMEM((strip, wide), bf16),
        pltpu.VMEM((replicas * piece, wide), bf16),
        pltpu.SemaphoreType.DMA((len(PIECES),)),
        pltpu.SemaphoreType.DMA((len(PIECES),)),
        pltpu.SemaphoreType.DMA((2, here)),
        pltpu.SemaphoreType.DMA((here,)),
        pltpu.SemaphoreType.DMA((here,)),
        pltpu.SemaphoreType.DMA((len(PIECES),)),
        pltpu.SemaphoreType.DMA((2,)),
        pltpu.SemaphoreType.DMA((6, 2)),
    ]
    result = pl.pallas_call(
        functools.partial(kernel, sizes),
        out_shape=jax.ShapeDtypeStruct((rows, wide), bf16),
        in_specs=[hbm] * 6,
        out_specs=hbm,
        scratch_shapes=scratch,
        compiler_params=pltpu.CompilerParams(
            collective_id=0, has_side_effects=True, vmem_limit_bytes=63 * 1024 * 1024
        ),
        cost_estimate=pl.CostEstimate(
            flops=6 * here * rows * wide * pixels, bytes_accessed=4 * rows * wide, transcendentals=0
        ),
    )(
        latents,
        target,
        base_weight[0].transpose(1, 0, 2),
        seeds,
        timesteps,
        time_table[0].T,
    )
    return result.astype(f32).reshape(9, channels, wide).transpose(1, 0, 2)[None]


def solution(mesh):
    in_specs = (
        P("tensor", "dp", None),
        P("tensor", "dp", None),
        P("section", "tensor", None, None),
        P("section"),
        P("dp"),
        P("section", None, "tensor"),
    )
    out_specs = P("section", "tensor", None, None)
    return jax.shard_map(body, mesh=mesh, in_specs=in_specs, out_specs=out_specs, check_vma=False)
```

```python
import functools

import jax
import jax.numpy as jnp
from jax import lax
from jax.experimental import pallas as pl
from jax.experimental.pallas import tpu as pltpu
from jax.sharding import PartitionSpec as P

GROUP = 20
RES = 16
MOD = 65521
PIECES = (32, 16)
SIDE = 4
MESH = pl.DeviceIdType.MESH


def below_mod(value):
    value = (value >> 16) * 15 + (value & 65535)
    value = (value >> 16) * 15 + (value & 65535)
    return jnp.where(value >= MOD, value - MOD, value)


def group_sums(values_list, group):
    rows, lanes = values_list[0].shape
    groups = rows // group
    parts = []
    for values in values_list:
        while values.shape[1] > 128:
            half = values.shape[1] // 2
            values = values[:, :half] + values[:, half:]
        for g in range(groups):
            first, last = g * group, (g + 1) * group
            start, end = first // 8 * 8, -(-last // 8) * 8
            total = None
            for row in range(start, end, 8):
                tile = values[row : row + 8]
                if row < first or row + 8 > last:
                    place = lax.broadcasted_iota(jnp.int32, tile.shape, 0) + row
                    tile = jnp.where((place >= first) & (place < last), tile, 0.0)
                total = tile if total is None else total + tile
            parts.append(jnp.sum(total, axis=0, keepdims=True))
    sums = jnp.sum(jnp.concatenate(parts, axis=0), axis=1, keepdims=True)
    place = lax.broadcasted_iota(jnp.int32, (rows, 1), 0)
    spread = []
    for index in range(len(values_list)):
        base = index * groups
        result = jnp.broadcast_to(sums[base : base + 1], (rows, 1))
        for g in range(1, groups):
            result = jnp.where(place >= g * group, sums[base + g : base + g + 1], result)
        spread.append(result)
    return spread


def tap_masks(pixels):
    place = lax.broadcasted_iota(jnp.int32, (1, pixels), 1)
    row, col = place // RES, place % RES
    return {-1: (row >= 1, col >= 1), 0: (None, None), 1: (row < RES - 1, col < RES - 1)}


def moved(values, offset):
    pixels = values.shape[1]
    return values if offset % pixels == 0 else pltpu.roll(values, (-offset) % pixels, axis=1)


def kernel(
    sizes,
    latents_hbm,
    target_hbm,
    base_hbm,
    seed_hbm,
    steps_hbm,
    table_hbm,
    out_ref,
    latents_ref,
    target_ref,
    base_ref,
    table_ref,
    seed_ref,
    steps_ref,
    load_sem,
    weight,
    weight_t,
    bias,
    part_send,
    part_recv,
    shift_send,
    shift_recv,
    grad_send,
    grad_recv,
    columns,
    normed,
    scale,
    slope,
    held,
    total,
    sum_send,
    sum_recv,
    own_sum,
    across_recv,
    across_sum,
    sum_done,
    down_sem,
    up_sem,
    part_sem,
    shift_sem,
    grad_sem,
    sum_sem,
    out_sem,
    send_sem,
    input_send,
    bias_before,
    bias_sem,
):
    replicas, sections, shards, latents_here, all_latents = sizes
    dp = lax.axis_index("dp")
    section = lax.axis_index("section")
    shard = lax.axis_index("tensor")
    channels, pixels = held.shape
    wide = weight.shape[1]
    last = sections - 1
    side = across_recv.shape[0]
    other_side = replicas // side
    x, y = dp // other_side, lax.rem(dp, other_side)
    chunks, start = [], 0
    for piece in PIECES:
        chunks.append((start, piece))
        start += piece * replicas

    loads = [
        pltpu.make_async_copy(source, place, load_sem.at[n])
        for n, (source, place) in enumerate(
            [
                (steps_hbm, steps_ref),
                (seed_hbm, seed_ref),
                (table_hbm, table_ref),
                (latents_hbm, latents_ref),
                (base_hbm, base_ref),
                (target_hbm, target_ref),
            ]
        )
    ]
    for load in loads:
        load.start()

    barrier = pltpu.get_barrier_semaphore()

    def greet(section_to, skip_own):
        for j in range(1 if skip_own else 0, shards):
            peer = lax.rem(shard + j, shards)
            pl.semaphore_signal(
                barrier,
                inc=1,
                device_id={"section": section_to, "tensor": peer},
                device_id_type=MESH,
            )

    @pl.when(section > 0)
    def _():
        greet(section - 1, False)

    @pl.when(section < last)
    def _():
        greet(section + 1, False)

    @pl.when(section == last)
    def _():
        greet(section, True)

    for j in range(1, replicas):
        pl.semaphore_signal(
            barrier, inc=1, device_id={"dp": lax.rem(dp + j, replicas)}, device_id_type=MESH
        )

    masks = tap_masks(pixels)
    count = float(GROUP * pixels)

    def wait_for(ref, sem):
        pltpu.make_async_copy(ref, ref, sem).wait()

    def send(source, place, sent, arrived, device):
        pltpu.make_async_remote_copy(
            src_ref=source,
            dst_ref=place,
            send_sem=sent,
            recv_sem=arrived,
            device_id=device,
            device_id_type=MESH,
        ).start()

    order = [j for j in (4, 3, 5, 2, 6, 1, 7, 0) if j < shards]
    order += [j for j in range(shards) if j not in order]

    def make_part(latent, peer):
        rows = pl.ds(pl.multiple_of(peer * channels, 16), channels)
        part_send[latent, peer] = jnp.dot(
            weight_t[rows], columns[latent], preferred_element_type=jnp.float32
        ).astype(jnp.bfloat16)

    def send_parts(latent):
        @pl.when(section < last)
        def _():
            for j in order:
                peer = lax.rem(shard + j, shards)
                make_part(latent, peer)
                send(
                    part_send.at[latent, peer],
                    part_recv.at[0, latent, shard],
                    send_sem.at[0, latent],
                    part_sem.at[0, latent],
                    {"section": section + 1, "tensor": peer},
                )

        @pl.when(section == last)
        def _():
            for j in order:
                peer = lax.rem(shard + j, shards)
                make_part(latent, peer)
                if j:
                    send(
                        part_send.at[latent, peer],
                        part_recv.at[1, latent, shard],
                        send_sem.at[0, latent],
                        part_sem.at[1, latent],
                        {"tensor": peer},
                    )
                else:
                    pltpu.make_async_copy(
                        part_send.at[latent, shard],
                        part_recv.at[1, latent, shard],
                        part_sem.at[1, latent],
                    ).start()

    def summed(phase, latent, start):
        result = start
        for j in range(shards):
            result = result + part_recv[phase, latent, j].astype(jnp.float32)
        return result.astype(jnp.bfloat16)

    def take(latent):
        @pl.when(section == 0)
        def _():
            held[...] = latents_ref[...].astype(jnp.float32)[:, latent]

        @pl.when(section > 0)
        def _():
            if latent == 0:
                wait_for(bias_before, bias_sem.at[1])
            wait_for(shift_recv.at[latent], shift_sem.at[latent])
            wait_for(part_recv.at[0, latent], part_sem.at[0, latent])
            start = shift_recv[latent].astype(jnp.float32) + bias_before[latent][:, 0:1]
            held[...] = summed(0, latent, start).astype(jnp.float32)

        input_send[latent] = held[...].astype(jnp.bfloat16)
        shift_send[latent] = held[...] + bias[latent][:, 0:1]

    def send_shift(latent):
        @pl.when(section < last)
        def _():
            send(
                input_send.at[latent],
                shift_recv.at[latent],
                send_sem.at[2, latent],
                shift_sem.at[latent],
                {"section": section + 1},
            )

    def activate(latent):
        shifted = shift_send[latent]
        (sums,) = group_sums([shifted], GROUP)
        center = shifted - sums / count
        (squares,) = group_sums([center * center], GROUP)
        factor = lax.rsqrt(squares / count + 1e-05)
        value = center * factor
        sigmoid = 1.0 / (1.0 + jnp.exp(-value))
        activation = (value * sigmoid).astype(jnp.bfloat16).astype(jnp.float32)
        for dj in (-1, 0, 1):
            across = moved(activation, dj)
            if dj:
                across = jnp.where(masks[dj][1], across, 0.0)
            for di in (-1, 0, 1):
                tap = (di + 1) * 3 + dj + 1
                both = moved(across, di * RES)
                if di:
                    both = jnp.where(masks[di][0], both, 0.0)
                columns[latent, tap * channels : (tap + 1) * channels] = both.astype(jnp.bfloat16)
        normed[latent] = value
        slope[latent] = sigmoid
        scale[latent] = jnp.broadcast_to(factor, (channels, 128))

    def emit(latent):
        send_parts(latent)
        sigmoid = slope[latent]
        slope[latent] = sigmoid * (1.0 + normed[latent] * (1.0 - sigmoid))

    loads[0].wait()
    loads[2].wait()
    loads[3].wait()
    table_step = lax.broadcasted_iota(jnp.int32, table_ref.shape, 1)
    table = table_ref[...].astype(jnp.float32)
    for latent in range(latents_here):
        picked = jnp.where(table_step == steps_ref[latent], table, 0.0)
        own_bias = jnp.broadcast_to(jnp.sum(picked, axis=1, keepdims=True), (channels, 128))
        bias[latent] = own_bias

    @pl.when(section == 0)
    def _():
        take(0)
        activate(0)

    for n in (1, 4, 5):
        loads[n].wait()
    seed = seed_ref[0]
    out_channel = lax.broadcasted_iota(jnp.int32, (8, wide), 1)
    out_part = below_mod(out_channel[0:1] * 32749)
    row_channel = lax.broadcasted_iota(jnp.int32, (channels, 128), 0) + shard * channels
    lane = lax.broadcasted_iota(jnp.int32, (channels, 128), 1)
    for tap in range(9):
        first_index = (row_channel * 9 + tap) * wide
        high = first_index >> 16
        low = high * 15 + (first_index & 65535)
        over = low >= MOD
        low = jnp.where(over, low - MOD, low)
        high = jnp.where(over, high + 1, high)
        row_part = below_mod(low * 32749 + high * 12345 + seed)
        for col in range(0, wide, 128):
            size = min(128, wide - col)
            mixed = row_part[:, :size] + out_part[:, col : col + size]
            mixed = jnp.where(low[:, :size] + lane[:, :size] >= MOD - col, mixed + 12345, mixed)
            mixed = jnp.where(mixed >= MOD, mixed - MOD, mixed)
            mixed = jnp.where(mixed >= MOD, mixed - MOD, mixed)
            noise = mixed.astype(jnp.float32) / 65521.0 - 0.5
            weight[tap * channels : (tap + 1) * channels, col : col + size] = (
                base_ref[tap, :, col : col + size].astype(jnp.float32) + 0.02 * noise
            ).astype(jnp.bfloat16)
    weight_t[...] = weight[...].T

    for s in range(sections):
        amount = replicas - 1 + shards * ((s > 0) + (s < last)) + (shards - 1) * (s == last)

        @pl.when(section == s)
        def _(amount=amount):
            pl.semaphore_wait(barrier, amount)

    @pl.when(section < last)
    def _():
        send(bias, bias_before, bias_sem.at[0], bias_sem.at[1], {"section": section + 1})

    @pl.when(section > 0)
    def _():
        take(0)
        send_shift(0)
        activate(0)

    @pl.when(section == 0)
    def _():
        send_shift(0)

    emit(0)
    for latent in range(1, latents_here):
        take(latent)
        send_shift(latent)
        activate(latent)
        emit(latent)

    grad_back = grad_send.at[1]
    grad_first = grad_send.at[0]

    for latent in range(latents_here):

        @pl.when(section == last)
        def _(latent=latent):
            wait_for(part_recv.at[1, latent], part_sem.at[1, latent])
            output = summed(1, latent, shift_send[latent]).astype(jnp.float32)
            grad_first[latent] = (
                (output - target_ref[...].astype(jnp.float32)[:, latent]) / float(all_latents)
            ).astype(jnp.bfloat16)
            for j in order:
                peer = lax.rem(shard + j, shards)
                if j:
                    send(
                        grad_first.at[latent],
                        grad_recv.at[latent, shard],
                        send_sem.at[3, latent],
                        grad_sem.at[latent],
                        {"tensor": peer},
                    )
                else:
                    pltpu.make_async_copy(
                        grad_first.at[latent], grad_recv.at[latent, shard], grad_sem.at[latent]
                    ).start()

    def added(ref, rows):
        result = ref[0, rows].astype(jnp.float32)
        for j in range(1, ref.shape[0]):
            result = result + ref[j, rows].astype(jnp.float32)
        return result.astype(jnp.bfloat16)

    def place_of(c, x_to, y_to, strip=False):
        start, piece = chunks[c]
        row = start + (x_to * other_side + y_to) * piece
        return pl.ds(pl.multiple_of(row, 16), piece * (other_side if strip else 1))

    def kept(c, strip=False):
        start, piece = chunks[c]
        scale_by = side if strip else replicas
        return pl.ds(start // scale_by, piece * (other_side if strip else 1))

    def around(size):
        return sorted(range(size), key=lambda j: -min(j, size - j))

    steps = [(i, j) for i in range(side) for j in range(other_side)]
    steps.sort(key=lambda ij: -min(ij[0], side - ij[0]) - 2 * min(ij[1], other_side - ij[1]))
    far_first = [
        (i + j, lax.rem(x + i, side) * other_side + lax.rem(y + j, other_side)) for i, j in steps
    ]

    def along_x(c):
        for j in around(side):
            to = lax.rem(x + j, side)
            source = sum_send.at[place_of(c, to, 0, True)]
            place = across_recv.at[x, kept(c, True)]
            if j:
                device = {"dp": to * other_side + y}
                send(source, place, send_sem.at[4, 0], sum_sem.at[c], device)
            else:
                pltpu.make_async_copy(source, place, sum_sem.at[c]).start()

    def along_y(c):
        start, piece = chunks[c]
        rows = kept(c, True)
        wait_for(across_recv.at[:, rows], sum_sem.at[c])
        across_sum[rows] = added(across_recv, rows)
        for j in around(other_side):
            to = lax.rem(y + j, other_side)
            row = pl.multiple_of(start // side + to * piece, 16)
            source = across_sum.at[pl.ds(row, piece)]
            place = sum_recv.at[y, kept(c)]
            if j:
                device = {"dp": x * other_side + to}
                send(source, place, send_sem.at[4, 1], down_sem.at[c], device)
            else:
                pltpu.make_async_copy(source, place, down_sem.at[c]).start()

    padding = sum_send.shape[0] - weight.shape[0]
    sum_send[pl.ds(weight.shape[0], padding)] = jnp.zeros((padding, wide), jnp.bfloat16)

    for latent in range(latents_here):
        wait_for(grad_recv.at[latent], grad_sem.at[latent])
        out_grad = grad_recv[latent].reshape(wide, pixels)

        @pl.when(section > 0)
        def _(latent=latent, out_grad=out_grad):
            spread = jnp.dot(weight[...], out_grad, preferred_element_type=jnp.float32)
            col_grad = None
            for dj in (-1, 0, 1):
                down = None
                for di in (-1, 0, 1):
                    tap = (di + 1) * 3 + dj + 1
                    term = spread[tap * channels : (tap + 1) * channels]
                    if di:
                        term = moved(jnp.where(masks[di][0], term, 0.0), -di * RES)
                    down = term if down is None else down + term
                if dj:
                    down = moved(jnp.where(masks[dj][1], down, 0.0), -dj)
                col_grad = down if col_grad is None else col_grad + down
            value = normed[latent]
            inner = col_grad * slope[latent]
            mean_inner, mean_both = group_sums([inner, inner * value], GROUP)
            in_grad = scale[latent][:, 0:1] * (
                inner - mean_inner / count - value * (mean_both / count)
            )
            grad_back[latent] = (
                grad_recv[latent, shard].astype(jnp.float32) + in_grad
            ).astype(jnp.bfloat16)
            for j in order:
                send(
                    grad_back.at[latent],
                    grad_recv.at[latent, shard],
                    send_sem.at[1, latent],
                    grad_sem.at[latent],
                    {
                        "section": section - 1,
                        "tensor": lax.rem(shard + j, shards),
                    },
                )

        for c, (start, piece) in enumerate(chunks):
            rows = pl.ds(start, min(piece * replicas, weight.shape[0] - start))
            part = lax.dot_general(
                columns[latent, rows],
                out_grad,
                (((1,), (1,)), ((), ())),
                preferred_element_type=jnp.float32,
            )
            if latent:
                part = total[rows] + part
            if latent < latents_here - 1:
                total[rows] = part
            else:
                sum_send[rows] = part.astype(jnp.bfloat16)
                along_x(c)

    @pl.when(section == 0)
    def _():
        for c in range(len(chunks)):
            along_y(c)
        for c in range(len(chunks)):
            rows = kept(c)
            wait_for(sum_recv.at[pl.ds(0, other_side), rows], down_sem.at[c])
            own_sum[rows] = added(sum_recv.at[pl.ds(0, other_side)], rows)
            place = sum_done.at[place_of(c, 0, dp)]
            for j, other in far_first:
                if j:
                    send(
                        own_sum.at[rows], place, send_sem.at[5, 0], out_sem.at[0], {"dp": other}
                    )
                else:
                    pltpu.make_async_copy(own_sum.at[rows], place, out_sem.at[0]).start()
        wait_for(sum_done, out_sem.at[0])
        wait_for(across_recv.at[pl.ds(0, side - 1)], send_sem.at[4, 0])
        wait_for(sum_recv.at[pl.ds(0, other_side - 1)], send_sem.at[4, 1])
        wait_for(sum_recv.at[pl.ds(0, replicas - 1)], send_sem.at[5, 0])

    @pl.when(section > 0)
    def _():
        def back_y(c):
            rows = kept(c)
            wait_for(sum_recv.at[pl.ds(0, other_side), rows], down_sem.at[c])
            own_sum[rows] = added(sum_recv.at[pl.ds(0, other_side)], rows)
            place = sum_done.at[place_of(c, x, y)]
            for j in around(other_side):
                if j:
                    device = {"dp": x * other_side + lax.rem(y + j, other_side)}
                    send(own_sum.at[rows], place, send_sem.at[5, 0], up_sem.at[c], device)
                else:
                    pltpu.make_async_copy(own_sum.at[rows], place, up_sem.at[c]).start()

        def back_x(c):
            mine = sum_done.at[place_of(c, x, 0, True)]
            wait_for(mine, up_sem.at[c])
            for j in around(side)[:-1]:
                device = {"dp": lax.rem(x + j, side) * other_side + y}
                send(mine, mine, send_sem.at[5, 1], out_sem.at[0], device)

        stages = (along_y, back_y, back_x)
        for step in range(len(chunks) + len(stages) - 1):
            for n in reversed(range(len(stages))):
                if 0 <= step - n < len(chunks):
                    stages[n](step - n)
        others = across_recv.at[pl.ds(0, side - 1)]
        wait_for(others, out_sem.at[0])
        wait_for(others, send_sem.at[4, 0])
        wait_for(others, send_sem.at[5, 1])
        for n in ((4, 1), (5, 0)):
            wait_for(sum_recv.at[pl.ds(0, other_side - 1)], send_sem.at[n])

    result = pltpu.make_async_copy(sum_done.at[pl.ds(0, out_ref.shape[0])], out_ref, out_sem.at[1])
    result.start()

    @pl.when(section < last)
    def _():
        wait_for(bias, bias_sem.at[0])

    for latent in range(latents_here):

        @pl.when(section < last)
        def _(latent=latent):
            wait_for(part_send.at[latent], send_sem.at[0, latent])
            wait_for(input_send.at[latent], send_sem.at[2, latent])

        @pl.when(section == last)
        def _(latent=latent):
            others = part_send.at[latent, pl.ds(0, shards - 1)]
            wait_for(others, send_sem.at[0, latent])
            wait_for(others, send_sem.at[3, latent])

        @pl.when(section > 0)
        def _(latent=latent):
            wait_for(part_send.at[latent], send_sem.at[1, latent])

    result.wait()


def body(latents, target, base_weight, seeds, timesteps, time_table):
    replicas, sections, shards = (lax.axis_size(name) for name in ("dp", "section", "tensor"))
    channels, latents_here, pixels = latents.shape
    wide = base_weight.shape[3]
    rows = 9 * channels
    piece = sum(PIECES)
    side = min(SIDE, replicas)
    strip = piece * (replicas // side)
    sizes = (replicas, sections, shards, latents_here, latents_here * replicas)
    hbm = pl.BlockSpec(memory_space=pltpu.HBM)
    bf16, f32 = jnp.bfloat16, jnp.float32
    here = latents_here
    scratch = [
        pltpu.VMEM((channels, here, pixels), bf16),
        pltpu.VMEM((channels, here, pixels), bf16),
        pltpu.VMEM((9, channels, wide), bf16),
        pltpu.VMEM(time_table.shape[:0:-1], bf16),
        pltpu.SMEM((1,), jnp.int32),
        pltpu.SMEM((here,), jnp.int32),
        pltpu.SemaphoreType.DMA((6,)),
        pltpu.VMEM((rows, wide), bf16),
        pltpu.VMEM((wide, rows), bf16),
        pltpu.VMEM((here, channels, 128), f32),
        pltpu.VMEM((here, shards, channels, pixels), bf16),
        pltpu.VMEM((2, here, shards, channels, pixels), bf16),
        pltpu.VMEM((here, channels, pixels), f32),
        pltpu.VMEM((here, channels, pixels), bf16),
        pltpu.VMEM((2, here, channels, pixels), bf16),
        pltpu.VMEM((here, shards, channels, pixels), bf16),
        pltpu.VMEM((here, rows, pixels), bf16),
        pltpu.VMEM((here, channels, pixels), f32),
        pltpu.VMEM((here, channels, 128), f32),
        pltpu.VMEM((here, channels, pixels), f32),
        pltpu.VMEM((channels, pixels), f32),
        pltpu.VMEM((rows, wide), f32),
        pltpu.VMEM((replicas * piece, wide), bf16),
        pltpu.VMEM((replicas, piece, wide), bf16),
        pltpu.VMEM((piece, wide), bf16),
        pltpu.VMEM((side, strip, wide), bf16),
        pltpu.VMEM((strip, wide), bf16),
        pltpu.VMEM((replicas * piece, wide), bf16),
        pltpu.SemaphoreType.DMA((len(PIECES),)),
        pltpu.SemaphoreType.DMA((len(PIECES),)),
        pltpu.SemaphoreType.DMA((2, here)),
        pltpu.SemaphoreType.DMA((here,)),
        pltpu.SemaphoreType.DMA((here,)),
        pltpu.SemaphoreType.DMA((len(PIECES),)),
        pltpu.SemaphoreType.DMA((2,)),
        pltpu.SemaphoreType.DMA((6, 2)),
        pltpu.VMEM((here, channels, pixels), bf16),
        pltpu.VMEM((here, channels, 128), f32),
        pltpu.SemaphoreType.DMA((2,)),
    ]
    result = pl.pallas_call(
        functools.partial(kernel, sizes),
        out_shape=jax.ShapeDtypeStruct((rows, wide), bf16),
        in_specs=[hbm] * 6,
        out_specs=hbm,
        scratch_shapes=scratch,
        compiler_params=pltpu.CompilerParams(
            collective_id=0, has_side_effects=True, vmem_limit_bytes=63 * 1024 * 1024
        ),
        cost_estimate=pl.CostEstimate(
            flops=6 * here * rows * wide * pixels, bytes_accessed=4 * rows * wide, transcendentals=0
        ),
    )(
        latents,
        target,
        base_weight[0].transpose(1, 0, 2),
        seeds,
        timesteps,
        time_table[0].T,
    )
    return result.astype(f32).reshape(9, channels, wide).transpose(1, 0, 2)[None]


def solution(mesh):
    in_specs = (
        P("tensor", "dp", None),
        P("tensor", "dp", None),
        P("section", "tensor", None, None),
        P("section"),
        P("dp"),
        P("section", None, "tensor"),
    )
    out_specs = P("section", "tensor", None, None)
    return jax.shard_map(body, mesh=mesh, in_specs=in_specs, out_specs=out_specs, check_vma=False)
```
